128 devices in a mesh: ctx: 8 (over x_lo, z), tp: 16 (over x_hi, y, core).
Axes of the slice: x: 4 (x_hi: 2, x_lo: 2; x = x_hi * 2 + x_lo), y: 4, z: 4, core: 2. Of those that a mesh axis runs over, the one named last changes fastest.
Arguments:
- in_gate: bfloat16 [4096, 4096], P('ctx', 'tp'), may hold values from -6 to 6
- value_stream: bfloat16 [4096, 4096], P('ctx', 'tp'), may hold values from -6 to 6
- out_gate: bfloat16 [4096, 4096], P('ctx', 'tp'), may hold values from -6 to 6
- residues: float32 [4096, 16], P('tp'), may hold values from -1.5 to 1.5
- decays: float32 [4096, 16], P('tp'), may hold values from 0.00024414062 to 0.05
- skip_gain: float32 [4096], P('tp'), may hold values from -3 to 3
- out_weight: bfloat16 [4096, 4096], P('tp'), may hold values from -0.09375 to 0.09375
Outputs:
- mixed: bfloat16 [4096, 4096], P(('ctx', 'tp'))
The draws below stay inside these ranges and needn't reach their ends.
All inputs are finite; a program needn't handle non-finite values.
Results may differ from the reference program's by a relative error of at most 0.017.
Values may be sent and summed in bfloat16 or wider, within the bound.
A program may use at most 128 MiB of HBM per device.

```python
import math
import jax
import jax.numpy as jnp
from jax import lax

D = 4096
MODES = 16
SEQ = 4096
BLOCK = 256


def shard_levels(stream_key, extent, shards, least, high):
    loudness, own = 1.0, jax.random.fold_in(stream_key, 6)
    for dim, blocks in shards:
        draws = jnp.exp(jax.random.uniform(jax.random.fold_in(own, dim), (blocks,), jnp.float32, least / len(shards), high / len(shards)))
        loudness = loudness * jnp.repeat(draws, extent[dim] // blocks).reshape([-1 if axis == dim else 1 for axis in range(len(extent))])
    return loudness


def scatter_about(own_key, dims, deviation, most, shards=(), dtype=jnp.bfloat16):
    factor_of = shard_levels(own_key, dims, shards, -0.22, 0.18) if shards else 1.0
    entries = jax.random.normal(own_key, dims, jnp.float32) * deviation * factor_of
    return jnp.minimum(jnp.maximum(entries, -most), most).astype(dtype)


def setup_inputs(seed: int = 0) -> dict:
    seeds = jax.random.split(jax.random.key(seed), 8)
    return {
        "in_gate": scatter_about(seeds[0], (SEQ, D), 1.0, 6.0, ((0, 8), (1, 16))),
        "value_stream": scatter_about(seeds[1], (SEQ, D), 1.0, 6.0, ((0, 8), (1, 16))),
        "out_gate": scatter_about(seeds[2], (SEQ, D), 1.0, 6.0, ((0, 8), (1, 16))),
        "residues": scatter_about(seeds[3], (D, MODES), 0.25, 1.5, ((0, 16),), jnp.float32),
        "decays": jnp.clip(jnp.exp(math.log(0.05) - 5.322034 * jax.random.uniform(seeds[4], (D, MODES), jnp.float32) ** shard_levels(seeds[4], (D, MODES), ((0, 16),), -0.2, 0.2)), 0.00024414062, 0.05),
        "skip_gain": scatter_about(seeds[5], (D,), 0.5, 3.0, ((0, 16),), jnp.float32),
        "out_weight": scatter_about(seeds[6], (D, D), D ** -0.5, 0.09375, ((0, 16),)),
    }


def modal_filter(block_res, block_dec, length):
    positions = jnp.arange(length).astype(jnp.float32)
    amplitude = block_res * jnp.sqrt(2.0 * block_dec)
    return lax.optimization_barrier(jnp.sum(amplitude[:, :, None] * jnp.exp(-block_dec[:, :, None] * positions[None, None, :]), axis=1))

def reference(in_gate, value_stream, out_gate, residues, decays, skip_gain, out_weight):
    product = (in_gate.astype(jnp.float32) * value_stream.astype(jnp.float32)).astype(jnp.bfloat16)
    group_width = 128
    groups = D // group_width
    signal = product.astype(jnp.float32).T.reshape(groups, group_width, SEQ)
    residue_blocks = residues.reshape(groups, group_width, MODES)
    dec_blocks = decays.reshape(groups, group_width, MODES)

    def convolve(pieces):
        block_signal, block_res, block_dec = pieces
        impulse = modal_filter(block_res, block_dec, SEQ)
        spectrum = jnp.fft.rfft(block_signal, n=2 * SEQ, axis=1) * jnp.fft.rfft(impulse, n=2 * SEQ, axis=1)
        return jnp.fft.irfft(spectrum, n=2 * SEQ, axis=1)[:, :SEQ]
    convolved = lax.map(convolve, (signal, residue_blocks, dec_blocks))
    convolved = convolved.reshape(D, SEQ).T
    gated = (out_gate.astype(jnp.float32) * (convolved + skip_gain * product.astype(jnp.float32))).astype(jnp.bfloat16)
    running = jnp.zeros((SEQ, D), jnp.float32)
    for block_index in range(D // BLOCK):
        lower = block_index * BLOCK
        partial_value = jnp.dot(gated[:, lower:lower + BLOCK], out_weight[lower:lower + BLOCK, :], preferred_element_type=jnp.float32)
        rounded = lax.optimization_barrier(partial_value.astype(jnp.bfloat16))
        running = running + rounded.astype(jnp.float32)
    return running.astype(jnp.bfloat16)
```

```python
import functools

import jax
import jax.numpy as jnp
from jax import lax
from jax.experimental import pallas as pl
from jax.experimental.pallas import tpu as pltpu
from jax.sharding import PartitionSpec as P

MESH = pl.DeviceIdType.MESH
F32 = jnp.float32
BF16 = jnp.bfloat16

LANES = 128
SUB = 8
YS = 4
PIECES = 8


def kernel(
    in_hbm, val_hbm, gate_hbm, res_ref, dec_ref, skip_ref, w_hbm, out_ref,
    ig, vs, og, w2, px, py, prefix, states, g_out, g2, part, rel, drt, com, x_out, x_in, acc,
    load_sem, st_send, st_recv, pair_send, pair_recv, rel_sem, drt_sem, com_sem, x_sem,
):
    tokens, chans = px.shape[1], px.shape[0] * LANES
    steps = tokens // SUB
    modes = res_ref.shape[0]
    n_ctx = states.shape[0]
    groups = chans // LANES
    rows = out_ref.shape[0]
    wide = part.shape[2]

    ctx = lax.axis_index("ctx")
    tp = lax.axis_index("tp")
    core = lax.rem(tp, 2)
    y = lax.rem(lax.div(tp, 2), YS)
    xh = lax.div(tp, 2 * YS)

    def device(ctx_i, xh_i, y_i, core_i):
        return (ctx_i, (xh_i * YS + y_i) * 2 + core_i)

    partner = device(ctx, xh, y, 1 - core)
    up = device(ctx, xh, lax.rem(y + 1, YS), core)
    down = device(ctx, xh, lax.rem(y + YS - 1, YS), core)
    across = device(ctx, 1 - xh, y, core)
    others = [(lax.rem(ctx + k, n_ctx), tp) for k in range(1, n_ctx)]

    barrier = pltpu.get_barrier_semaphore()
    peers = [partner, up, down, across] + others
    for peer in peers:
        pl.semaphore_signal(barrier, inc=1, device_id=peer, device_id_type=MESH)

    loads = [
        pltpu.make_async_copy(in_hbm, ig, load_sem.at[0]),
        pltpu.make_async_copy(val_hbm, vs, load_sem.at[1]),
        pltpu.make_async_copy(gate_hbm, og, load_sem.at[2]),
        pltpu.make_async_copy(w_hbm, w2.at[pl.ds(0, chans)], load_sem.at[3]),
    ]
    for load in loads:
        load.start()
    loads[0].wait()
    loads[1].wait()

    for g in range(groups):
        lanes = pl.ds(g * LANES, LANES)
        product = (ig[:, lanes].astype(F32) * vs[:, lanes].astype(F32)).astype(BF16)
        px[g] = product.astype(F32)

    def spread(row):
        return jnp.broadcast_to(row, (SUB, LANES))

    position = lax.broadcasted_iota(jnp.int32, (SUB, LANES), 0)
    place = position.astype(F32)

    def group_decay(g):
        decay = dec_ref[:, pl.ds(g * LANES, LANES)]
        return decay, jnp.exp(-decay)

    for g in range(groups):
        lanes = pl.ds(g * LANES, LANES)
        decay, step_factor = group_decay(g)
        factors = [spread(step_factor[m : m + 1]) for m in range(modes)]

        def advance(i, held, factors=factors, g=g):
            x = px[g, pl.ds(i, SUB, stride=steps), :]
            return tuple(f * s + x for f, s in zip(factors, held))

        zero = jnp.zeros((SUB, LANES), F32)
        ends = lax.fori_loop(0, steps, advance, (zero,) * modes, unroll=8)
        for m in range(modes):
            rate = spread(decay[m : m + 1])
            tail = jnp.exp(-rate * ((SUB - 1 - place) * steps))
            states[ctx, m : m + 1, lanes] = jnp.sum(tail * ends[m], axis=0, keepdims=True)
            scan = jnp.where(position >= 1, pltpu.roll(ends[m], 1, 0), 0.0)
            for hop in (1, 2, 4):
                weight = jnp.where(position >= hop, jnp.exp(-rate * (hop * steps)), 0.0)
                scan = scan + weight * pltpu.roll(scan, hop, 0)
            prefix[g, m] = scan

    pl.semaphore_wait(barrier, len(peers))
    state_copies = []
    for k, peer in enumerate(others):
        copy = pltpu.make_async_remote_copy(
            src_ref=states.at[ctx], dst_ref=states.at[ctx],
            send_sem=st_send.at[k], recv_sem=st_recv.at[k],
            device_id=peer, device_id_type=MESH,
        )
        copy.start()
        state_copies.append(copy)
    w_copy = pltpu.make_async_remote_copy(
        src_ref=w_hbm, dst_ref=w2.at[pl.ds(chans, chans)],
        send_sem=pair_send.at[0], recv_sem=pair_recv.at[0],
        device_id=partner, device_id_type=MESH,
    )
    w_copy.start()

    for g in range(groups):
        lanes = pl.ds(g * LANES, LANES)
        decay, step_factor = group_decay(g)
        amplitude = res_ref[:, lanes] * jnp.sqrt(2.0 * decay)
        factors = [spread(step_factor[m : m + 1]) for m in range(modes)]
        gains = [spread(amplitude[m : m + 1]) for m in range(modes)]

        def convolve(i, held, factors=factors, gains=gains, g=g):
            rows_i = pl.ds(i, SUB, stride=steps)
            x = px[g, rows_i, :]
            held = tuple(f * s + x for f, s in zip(factors, held))
            terms = [r * s for r, s in zip(gains, held)]
            while len(terms) > 1:
                terms = [terms[j] + terms[j + 1] for j in range(0, len(terms), 2)]
            py[g, rows_i, :] = terms[0]
            return held

        lax.fori_loop(0, steps, convolve, tuple(prefix[g, m] for m in range(modes)), unroll=4)

    for copy in state_copies:
        copy.wait_recv()

    for g in range(groups):
        lanes = pl.ds(g * LANES, LANES)
        decay, step_factor = group_decay(g)
        amplitude = res_ref[:, lanes] * jnp.sqrt(2.0 * decay)
        block_factor = jnp.exp(-decay * float(tokens))
        carried = jnp.zeros((modes, LANES), F32)
        for i in range(n_ctx - 1):
            carried = jnp.where(i < ctx, block_factor * carried + states[i, :, lanes], carried)
        carried = carried * amplitude
        factors = [spread(step_factor[m : m + 1]) for m in range(modes)]
        fades = tuple(
            spread(carried[m : m + 1]) * jnp.exp(-spread(decay[m : m + 1]) * (place * steps + 1.0))
            for m in range(modes)
        )

        def extend(i, fades, factors=factors, g=g):
            rows_i = pl.ds(i, SUB, stride=steps)
            terms = list(fades)
            while len(terms) > 1:
                terms = [terms[j] + terms[j + 1] for j in range(0, len(terms), 2)]
            py[g, rows_i, :] = py[g, rows_i, :] + terms[0]
            return tuple(f * v for f, v in zip(factors, fades))

        lax.fori_loop(0, steps, extend, fades, unroll=4)

    loads[2].wait()

    def gated_rows(block, g):
        at = pl.ds(pl.multiple_of(block * rows, rows), rows)
        lanes = pl.ds(g * LANES, LANES)
        gate = og[at, lanes].astype(F32)
        return (gate * (py[g, at, :] + skip_ref[:, lanes] * px[g, at, :])).astype(BF16)

    def target_block(r, q, core_i):
        xh_t = lax.rem(xh + q, 2)
        return (xh_t * YS + lax.rem(y + r, YS)) * 2 + core_i

    for r in range(YS):
        for q in range(2):
            for g in range(groups):
                g_out[pl.ds((2 * r + q) * rows, rows), pl.ds(g * LANES, LANES)] = gated_rows(
                    target_block(r, q, 1 - core), g
                )
    g_copy = pltpu.make_async_remote_copy(
        src_ref=g_out, dst_ref=g2.at[:, pl.ds(chans, chans)],
        send_sem=pair_send.at[1], recv_sem=pair_recv.at[1],
        device_id=partner, device_id_type=MESH,
    )
    g_copy.start()
    for r in range(YS):
        for q in range(2):
            for g in range(groups):
                g2[pl.ds((2 * r + q) * rows, rows), pl.ds(g * LANES, LANES)] = gated_rows(
                    target_block(r, q, core), g
                )
    loads[3].wait()
    w_copy.wait_recv()
    g_copy.wait_recv()

    pair = 2 * rows

    def block_rows(r):
        return pl.ds(r * pair, pair)

    def sends(p, odd):
        near, far, off, back = (3, 2, down, up) if odd else (1, 2, up, down)
        rel_copy = functools.partial(
            pltpu.make_async_remote_copy,
            src_ref=part.at[p, block_rows(far)], dst_ref=rel.at[p],
            send_sem=rel_sem.at[0, p], recv_sem=rel_sem.at[1, p],
            device_id=off, device_id_type=MESH,
        )
        drt_copy = functools.partial(
            pltpu.make_async_remote_copy,
            src_ref=part.at[p, block_rows(4 - near)], dst_ref=drt.at[p],
            send_sem=drt_sem.at[0, p], recv_sem=drt_sem.at[1, p],
            device_id=back, device_id_type=MESH,
        )
        com_copy = functools.partial(
            pltpu.make_async_remote_copy,
            src_ref=part.at[p, block_rows(near)], dst_ref=com.at[p],
            send_sem=com_sem.at[0, p], recv_sem=com_sem.at[1, p],
            device_id=off, device_id_type=MESH,
        )
        x_copy = functools.partial(
            pltpu.make_async_remote_copy,
            src_ref=x_out.at[p], dst_ref=x_in.at[p],
            send_sem=x_sem.at[0, p], recv_sem=x_sem.at[1, p],
            device_id=across, device_id_type=MESH,
        )
        return near, rel_copy, drt_copy, com_copy, x_copy

    def multiply(j, carry):
        for odd in (0, 1):
            p = 2 * j + odd
            cols = pl.ds(pl.multiple_of(p * wide, wide), wide)
            part[p] = jnp.dot(g2[...], w2[:, cols], preferred_element_type=F32).astype(BF16)
            _, rel_copy, drt_copy, _, _ = sends(p, odd)
            rel_copy().start()
            drt_copy().start()
        return carry

    lax.fori_loop(0, PIECES // 2, multiply, 0)

    def relay(j, carry):
        for odd in (0, 1):
            p = 2 * j + odd
            near, rel_copy, _, com_copy, _ = sends(p, odd)
            rel_copy().wait_recv()
            at = block_rows(near)
            part[p, at] = (part[p, at].astype(F32) + rel[p].astype(F32)).astype(BF16)
            com_copy().start()
        return carry

    lax.fori_loop(0, PIECES // 2, relay, 0)

    def gather(j, carry):
        for odd in (0, 1):
            p = 2 * j + odd
            _, _, drt_copy, com_copy, x_copy = sends(p, odd)
            drt_copy().wait_recv()
            com_copy().wait_recv()
            total = part[p, block_rows(0)].astype(F32) + drt[p].astype(F32) + com[p].astype(F32)
            x_out[p] = total[rows:].astype(BF16)
            x_copy().start()
            acc[p] = total[:rows]
        return carry

    lax.fori_loop(0, PIECES // 2, gather, 0)

    def finish(j, carry):
        for odd in (0, 1):
            p = 2 * j + odd
            _, rel_copy, drt_copy, com_copy, x_copy = sends(p, odd)
            x_copy().wait_recv()
            cols = pl.ds(pl.multiple_of(p * wide, wide), wide)
            out_ref[:, cols] = (acc[p] + x_in[p].astype(F32)).astype(BF16)
            rel_copy().wait_send()
            drt_copy().wait_send()
            com_copy().wait_send()
            x_copy().wait_send()
        return carry

    lax.fori_loop(0, PIECES // 2, finish, 0)
    for copy in state_copies:
        copy.wait_send()
    w_copy.wait_send()
    g_copy.wait_send()


def body(n_ctx, n_tp, in_gate, value_stream, out_gate, residues, decays, skip_gain, out_weight):
    tokens, chans = in_gate.shape
    modes = residues.shape[1]
    width = out_weight.shape[1]
    rows = tokens // n_tp
    wide = width // PIECES
    groups = chans // LANES
    any_space = pl.BlockSpec(memory_space=pl.ANY)
    vmem = pl.BlockSpec(memory_space=pltpu.VMEM)
    dma = pltpu.SemaphoreType.DMA
    return pl.pallas_call(
        kernel,
        out_shape=jax.ShapeDtypeStruct((rows, width), BF16),
        in_specs=[any_space] * 3 + [vmem] * 3 + [any_space],
        out_specs=vmem,
        scratch_shapes=[
            pltpu.VMEM((tokens, chans), BF16),
            pltpu.VMEM((tokens, chans), BF16),
            pltpu.VMEM((tokens, chans), BF16),
            pltpu.VMEM((2 * chans, width), BF16),
            pltpu.VMEM((groups, tokens, LANES), F32),
            pltpu.VMEM((groups, tokens, LANES), F32),
            pltpu.VMEM((groups, modes, SUB, LANES), F32),
            pltpu.VMEM((n_ctx, modes, chans), F32),
            pltpu.VMEM((tokens // 2, chans), BF16),
            pltpu.VMEM((tokens // 2, 2 * chans), BF16),
            pltpu.VMEM((PIECES, tokens // 2, wide), BF16),
            pltpu.VMEM((PIECES, 2 * rows, wide), BF16),
            pltpu.VMEM((PIECES, 2 * rows, wide), BF16),
            pltpu.VMEM((PIECES, 2 * rows, wide), BF16),
            pltpu.VMEM((PIECES, rows, wide), BF16),
            pltpu.VMEM((PIECES, rows, wide), BF16),
            pltpu.VMEM((PIECES, rows, wide), F32),
            dma((4,)),
            dma((n_ctx - 1,)),
            dma((n_ctx - 1,)),
            dma((2,)),
            dma((2,)),
            dma((2, PIECES)),
            dma((2, PIECES)),
            dma((2, PIECES)),
            dma((2, PIECES)),
        ],
        compiler_params=pltpu.CompilerParams(
            collective_id=0, has_side_effects=True, vmem_limit_bytes=48 * 1024 * 1024
        ),
        cost_estimate=pl.CostEstimate(
            flops=2 * tokens * chans * width, bytes_accessed=4 * 1024 * 1024, transcendentals=0
        ),
    )(
        in_gate, value_stream, out_gate, residues.T, decays.T,
        skip_gain.reshape(1, chans), out_weight,
    )


def solution(mesh):
    n_ctx, n_tp = mesh.shape["ctx"], mesh.shape["tp"]
    in_specs = (
        P("ctx", "tp"),
        P("ctx", "tp"),
        P("ctx", "tp"),
        P("tp", None),
        P("tp", None),
        P("tp"),
        P("tp", None),
    )
    out_specs = P(("ctx", "tp"), None)
    return jax.shard_map(
        functools.partial(body, n_ctx, n_tp),
        mesh=mesh, in_specs=in_specs, out_specs=out_specs, check_vma=False,
    )
```

```python
import functools

import jax
import jax.numpy as jnp
from jax import lax
from jax.experimental import pallas as pl
from jax.experimental.pallas import tpu as pltpu
from jax.sharding import PartitionSpec as P

MESH = pl.DeviceIdType.MESH
F32 = jnp.float32
BF16 = jnp.bfloat16

LANES = 128
SUB = 8
YS = 4
X_PIECES, Y_PIECES = 7, 9


def kernel(
    in_hbm, val_hbm, gate_hbm, res_hbm, dec_hbm, skip_hbm, w_hbm, out_ref,
    res_ref, dec_ref, skip_ref, ig, vs, og, w2, px, py, prefix, states, g_out, g2, part,
    x_in, x_rel, x_drt, x_com, y_rel, y_drt, y_com, y_out, y_in, acc,
    load_sem, st_send, st_recv, pair_send, pair_recv, x_sem, y_sem,
):
    tokens, chans = px.shape[1], px.shape[0] * LANES
    steps = tokens // SUB
    modes = res_ref.shape[0]
    n_ctx = states.shape[0]
    groups = chans // LANES
    rows = out_ref.shape[0]
    wide = part.shape[3]

    ctx = lax.axis_index("ctx")
    tp = lax.axis_index("tp")
    core = lax.rem(tp, 2)
    y = lax.rem(lax.div(tp, 2), YS)
    xh = lax.div(tp, 2 * YS)

    def device(ctx_i, xh_i, y_i, core_i):
        return (ctx_i, (xh_i * YS + y_i) * 2 + core_i)

    partner = device(ctx, xh, y, 1 - core)
    up = device(ctx, xh, lax.rem(y + 1, YS), core)
    down = device(ctx, xh, lax.rem(y + YS - 1, YS), core)
    across = device(ctx, 1 - xh, y, core)
    others = [(lax.rem(ctx + k, n_ctx), tp) for k in range(1, n_ctx)]

    barrier = pltpu.get_barrier_semaphore()
    peers = [partner, up, down, across] + others
    for peer in peers:
        pl.semaphore_signal(barrier, inc=1, device_id=peer, device_id_type=MESH)

    small = [
        pltpu.make_async_copy(dec_hbm, dec_ref, load_sem.at[4]),
        pltpu.make_async_copy(res_hbm, res_ref, load_sem.at[5]),
        pltpu.make_async_copy(skip_hbm, skip_ref, load_sem.at[6]),
    ]
    loads = [
        pltpu.make_async_copy(in_hbm, ig, load_sem.at[0]),
        pltpu.make_async_copy(val_hbm, vs, load_sem.at[1]),
        pltpu.make_async_copy(gate_hbm, og, load_sem.at[2]),
        pltpu.make_async_copy(w_hbm, w2.at[pl.ds(0, chans)], load_sem.at[3]),
    ]
    for load in loads[:2] + small + loads[2:]:
        load.start()
    loads[0].wait()
    loads[1].wait()

    for g in range(groups):
        lanes = pl.ds(g * LANES, LANES)
        product = (ig[:, lanes].astype(F32) * vs[:, lanes].astype(F32)).astype(BF16)
        px[g] = product.astype(F32)

    def spread(row):
        return jnp.broadcast_to(row, (SUB, LANES))

    position = lax.broadcasted_iota(jnp.int32, (SUB, LANES), 0)
    place = position.astype(F32)

    def group_decay(g):
        decay = dec_ref[:, pl.ds(g * LANES, LANES)]
        return decay, jnp.exp(-decay)

    for load in small:
        load.wait()

    for g in range(groups):
        lanes = pl.ds(g * LANES, LANES)
        decay, step_factor = group_decay(g)
        factors = [spread(step_factor[m : m + 1]) for m in range(modes)]

        def advance(i, held, factors=factors, g=g):
            x = px[g, pl.ds(i, SUB, stride=steps), :]
            return tuple(f * s + x for f, s in zip(factors, held))

        zero = jnp.zeros((SUB, LANES), F32)
        ends = lax.fori_loop(0, steps, advance, (zero,) * modes, unroll=8)
        for m in range(modes):
            rate = spread(decay[m : m + 1])
            tail = jnp.exp(-rate * ((SUB - 1 - place) * steps))
            states[ctx, m : m + 1, lanes] = jnp.sum(tail * ends[m], axis=0, keepdims=True)
            scan = jnp.where(position >= 1, pltpu.roll(ends[m], 1, 0), 0.0)
            for hop in (1, 2, 4):
                weight = jnp.where(position >= hop, jnp.exp(-rate * (hop * steps)), 0.0)
                scan = scan + weight * pltpu.roll(scan, hop, 0)
            prefix[g, m] = scan

    pl.semaphore_wait(barrier, len(peers))
    state_copies = []
    for k, peer in enumerate(others):
        copy = pltpu.make_async_remote_copy(
            src_ref=states.at[ctx], dst_ref=states.at[ctx],
            send_sem=st_send.at[k], recv_sem=st_recv.at[k],
            device_id=peer, device_id_type=MESH,
        )
        copy.start()
        state_copies.append(copy)
    w_copy = pltpu.make_async_remote_copy(
        src_ref=w_hbm, dst_ref=w2.at[pl.ds(chans, chans)],
        send_sem=pair_send.at[0], recv_sem=pair_recv.at[0],
        device_id=partner, device_id_type=MESH,
    )
    w_copy.start()

    for g in range(groups):
        lanes = pl.ds(g * LANES, LANES)
        decay, step_factor = group_decay(g)
        amplitude = res_ref[:, lanes] * jnp.sqrt(2.0 * decay)
        factors = [spread(step_factor[m : m + 1]) for m in range(modes)]
        gains = [spread(amplitude[m : m + 1]) for m in range(modes)]

        def convolve(i, held, factors=factors, gains=gains, g=g):
            rows_i = pl.ds(i, SUB, stride=steps)
            x = px[g, rows_i, :]
            held = tuple(f * s + x for f, s in zip(factors, held))
            terms = [r * s for r, s in zip(gains, held)]
            while len(terms) > 1:
                terms = [terms[j] + terms[j + 1] for j in range(0, len(terms), 2)]
            py[g, rows_i, :] = terms[0]
            return held

        lax.fori_loop(0, steps, convolve, tuple(prefix[g, m] for m in range(modes)), unroll=4)

    for copy in state_copies:
        copy.wait_recv()

    for g in range(groups):
        lanes = pl.ds(g * LANES, LANES)
        decay, step_factor = group_decay(g)
        amplitude = res_ref[:, lanes] * jnp.sqrt(2.0 * decay)
        block_factor = jnp.exp(-decay * float(tokens))
        carried = jnp.zeros((modes, LANES), F32)
        for i in range(n_ctx - 1):
            carried = jnp.where(i < ctx, block_factor * carried + states[i, :, lanes], carried)
        carried = carried * amplitude
        factors = [spread(step_factor[m : m + 1]) for m in range(modes)]
        fades = tuple(
            spread(carried[m : m + 1]) * jnp.exp(-spread(decay[m : m + 1]) * (place * steps + 1.0))
            for m in range(modes)
        )

        def extend(i, fades, factors=factors, g=g):
            rows_i = pl.ds(i, SUB, stride=steps)
            terms = list(fades)
            while len(terms) > 1:
                terms = [terms[j] + terms[j + 1] for j in range(0, len(terms), 2)]
            py[g, rows_i, :] = py[g, rows_i, :] + terms[0]
            return tuple(f * v for f, v in zip(factors, fades))

        lax.fori_loop(0, steps, extend, fades, unroll=4)

    loads[2].wait()

    def gated_rows(block, g):
        at = pl.ds(pl.multiple_of(block * rows, rows), rows)
        lanes = pl.ds(g * LANES, LANES)
        gate = og[at, lanes].astype(F32)
        return (gate * (py[g, at, :] + skip_ref[:, lanes] * px[g, at, :])).astype(BF16)

    def target_block(r, q, core_i):
        xh_t = lax.rem(xh + q, 2)
        return (xh_t * YS + lax.rem(y + r, YS)) * 2 + core_i

    for r in range(YS):
        for q in range(2):
            for g in range(groups):
                g_out[pl.ds((q * YS + r) * rows, rows), pl.ds(g * LANES, LANES)] = gated_rows(
                    target_block(r, q, 1 - core), g
                )
    g_copy = pltpu.make_async_remote_copy(
        src_ref=g_out, dst_ref=g2.at[:, pl.ds(chans, chans)],
        send_sem=pair_send.at[1], recv_sem=pair_recv.at[1],
        device_id=partner, device_id_type=MESH,
    )
    g_copy.start()
    for r in range(YS):
        for q in range(2):
            for g in range(groups):
                g2[pl.ds((q * YS + r) * rows, rows), pl.ds(g * LANES, LANES)] = gated_rows(
                    target_block(r, q, core), g
                )
    loads[3].wait()
    w_copy.wait_recv()
    g_copy.wait_recv()

    half = YS * rows
    n_x, n_y = x_in.shape[0], y_in.shape[0]

    def send(src, dst, sems, k, to):
        return pltpu.make_async_remote_copy(
            src_ref=src, dst_ref=dst, send_sem=sems.at[0, k], recv_sem=sems.at[1, k],
            device_id=to, device_id_type=MESH,
        )

    def neighbour(turn):
        return device(ctx, xh, lax.rem(y + 1 + 2 * turn, YS), core)

    def block(r):
        return pl.ds(r * rows, rows)

    def y_first(k):
        turn = lax.rem(k, 2)
        p = n_x + k
        src = part.at[p]
        return (
            p, 1 + 2 * turn,
            functools.partial(send, src.at[:, block(2)], y_rel.at[k], y_sem.at[0], k, neighbour(turn)),
            functools.partial(send, src.at[:, block(3 - 2 * turn)], y_drt.at[k], y_sem.at[1], k, neighbour(1 - turn)),
            functools.partial(send, src.at[:, block(1 + 2 * turn)], y_com.at[k], y_sem.at[2], k, neighbour(turn)),
            functools.partial(send, y_out.at[k], y_in.at[k], y_sem.at[3], k, across),
        )

    def x_first(k):
        turn = lax.rem(k + 1, 2)
        src = part.at[k, 0]
        return (
            1 + 2 * turn,
            functools.partial(send, src.at[block(2)], x_rel.at[k], x_sem.at[0], k, neighbour(turn)),
            functools.partial(send, src.at[block(3 - 2 * turn)], x_drt.at[k], x_sem.at[1], k, neighbour(1 - turn)),
            functools.partial(send, src.at[block(1 + 2 * turn)], x_com.at[k], x_sem.at[2], k, neighbour(turn)),
            functools.partial(send, part.at[k, 1], x_in.at[k], x_sem.at[3], k, across),
        )

    def columns(p):
        return pl.ds(pl.multiple_of(p * wide, wide), wide)

    def multiply(p):
        product = jnp.dot(g2[...], w2[:, columns(p)], preferred_element_type=F32)
        part[p] = product.astype(BF16).reshape(2, half, wide)

    def stage(x_step, y_step):
        def both(k, carry):
            x_step(k)
            y_step(k)
            return carry

        def one(k, carry):
            (x_step if n_x > n_y else y_step)(k)
            return carry

        lax.fori_loop(0, min(n_x, n_y), both, 0)
        lax.fori_loop(min(n_x, n_y), max(n_x, n_y), one, 0)

    def x_start(k):
        multiply(k)
        x_first(k)[4]().start()

    def y_start(k):
        multiply(n_x + k)
        _, _, rel, drt, _, _ = y_first(k)
        rel().start()
        drt().start()

    stage(x_start, y_start)

    def x_second(k):
        _, rel, drt, _, cross = x_first(k)
        cross().wait_recv()
        part[k, 0] = (part[k, 0].astype(F32) + x_in[k].astype(F32)).astype(BF16)
        rel().start()
        drt().start()

    def y_second(k):
        p, near, rel, _, com, _ = y_first(k)
        rel().wait_recv()
        part[p, :, block(near)] = (part[p, :, block(near)].astype(F32) + y_rel[k].astype(F32)).astype(BF16)
        com().start()

    stage(x_second, y_second)

    def x_third(k):
        near, rel, _, com, _ = x_first(k)
        rel().wait_recv()
        part[k, 0, block(near)] = (part[k, 0, block(near)].astype(F32) + x_rel[k].astype(F32)).astype(BF16)
        com().start()

    def y_third(k):
        p, _, _, drt, com, cross = y_first(k)
        drt().wait_recv()
        com().wait_recv()
        total = part[p, :, block(0)].astype(F32) + y_drt[k].astype(F32) + y_com[k].astype(F32)
        y_out[k] = total[1].astype(BF16)
        cross().start()
        acc[k] = total[0]

    stage(x_third, y_third)

    def x_last(k):
        _, rel, drt, com, cross = x_first(k)
        drt().wait_recv()
        com().wait_recv()
        total = part[k, 0, block(0)].astype(F32) + x_drt[k].astype(F32) + x_com[k].astype(F32)
        out_ref[:, columns(k)] = total.astype(BF16)
        for copy in (rel, drt, com, cross):
            copy().wait_send()

    def y_last(k):
        p, _, rel, drt, com, cross = y_first(k)
        cross().wait_recv()
        out_ref[:, columns(p)] = (acc[k] + y_in[k].astype(F32)).astype(BF16)
        for copy in (rel, drt, com, cross):
            copy().wait_send()

    stage(x_last, y_last)
    for copy in state_copies:
        copy.wait_send()
    w_copy.wait_send()
    g_copy.wait_send()


def body(n_ctx, n_tp, in_gate, value_stream, out_gate, residues, decays, skip_gain, out_weight):
    tokens, chans = in_gate.shape
    modes = residues.shape[1]
    width = out_weight.shape[1]
    rows = tokens // n_tp
    wide = width // (X_PIECES + Y_PIECES)
    groups = chans // LANES
    hbm = pl.BlockSpec(memory_space=pltpu.HBM)
    vmem = pl.BlockSpec(memory_space=pltpu.VMEM)
    dma = pltpu.SemaphoreType.DMA
    return pl.pallas_call(
        kernel,
        out_shape=jax.ShapeDtypeStruct((rows, width), BF16),
        in_specs=[hbm] * 7,
        out_specs=vmem,
        scratch_shapes=[
            pltpu.VMEM((modes, chans), F32),
            pltpu.VMEM((modes, chans), F32),
            pltpu.VMEM((1, chans), F32),
            pltpu.VMEM((tokens, chans), BF16),
            pltpu.VMEM((tokens, chans), BF16),
            pltpu.VMEM((tokens, chans), BF16),
            pltpu.VMEM((2 * chans, width), BF16),
            pltpu.VMEM((groups, tokens, LANES), F32),
            pltpu.VMEM((groups, tokens, LANES), F32),
            pltpu.VMEM((groups, modes, SUB, LANES), F32),
            pltpu.VMEM((n_ctx, modes, chans), F32),
            pltpu.VMEM((tokens // 2, chans), BF16),
            pltpu.VMEM((tokens // 2, 2 * chans), BF16),
            pltpu.VMEM((X_PIECES + Y_PIECES, 2, YS * rows, wide), BF16),
            pltpu.VMEM((X_PIECES, YS * rows, wide), BF16),
            pltpu.VMEM((X_PIECES, rows, wide), BF16),
            pltpu.VMEM((X_PIECES, rows, wide), BF16),
            pltpu.VMEM((X_PIECES, rows, wide), BF16),
            pltpu.VMEM((Y_PIECES, 2, rows, wide), BF16),
            pltpu.VMEM((Y_PIECES, 2, rows, wide), BF16),
            pltpu.VMEM((Y_PIECES, 2, rows, wide), BF16),
            pltpu.VMEM((Y_PIECES, rows, wide), BF16),
            pltpu.VMEM((Y_PIECES, rows, wide), BF16),
            pltpu.VMEM((Y_PIECES, rows, wide), F32),
            dma((7,)),
            dma((n_ctx - 1,)),
            dma((n_ctx - 1,)),
            dma((2,)),
            dma((2,)),
            dma((4, 2, X_PIECES)),
            dma((4, 2, Y_PIECES)),
        ],
        compiler_params=pltpu.CompilerParams(
            collective_id=0, has_side_effects=True, vmem_limit_bytes=62 * 1024 * 1024
        ),
        cost_estimate=pl.CostEstimate(
            flops=2 * tokens * chans * width, bytes_accessed=4 * 1024 * 1024, transcendentals=0
        ),
    )(
        in_gate, value_stream, out_gate, residues.T, decays.T,
        skip_gain.reshape(1, chans), out_weight,
    )


def solution(mesh):
    n_ctx, n_tp = mesh.shape["ctx"], mesh.shape["tp"]
    in_specs = (
        P("ctx", "tp"),
        P("ctx", "tp"),
        P("ctx", "tp"),
        P("tp", None),
        P("tp", None),
        P("tp"),
        P("tp", None),
    )
    out_specs = P(("ctx", "tp"), None)
    return jax.shard_map(
        functools.partial(body, n_ctx, n_tp),
        mesh=mesh, in_specs=in_specs, out_specs=out_specs, check_vma=False,
    )
```

```python
import functools

import jax
import jax.numpy as jnp
from jax import lax
from jax.experimental import pallas as pl
from jax.experimental.pallas import tpu as pltpu
from jax.sharding import PartitionSpec as P

MESH = pl.DeviceIdType.MESH
F32 = jnp.float32
BF16 = jnp.bfloat16

LANES = 128
SUB = 8
YS = 4
X_PIECES, Y_PIECES = 7, 9

SCHEDULE = (('y', 0, 0), ('x', 0, 0), ('y', 1, 0), ('x', 1, 0), ('y', 2, 0), ('x', 2, 0), ('y', 3, 0), ('x', 3, 0), ('y', 4, 0), ('x', 4, 0), ('y', 5, 0), ('d', 5, 0), ('y', 6, 0), ('d', 6, 0), ('y', 7, 0), ('y', 8, 0), ('y', 0, 1), ('y', 1, 1), ('x', 0, 1), ('y', 2, 1), ('y', 3, 1), ('x', 1, 1), ('y', 4, 1), ('y', 5, 1), ('x', 2, 1), ('y', 6, 1), ('y', 7, 1), ('x', 3, 1), ('y', 8, 1), ('y', 0, 2), ('x', 4, 1), ('y', 1, 2), ('x', 0, 2), ('y', 2, 2), ('y', 3, 2), ('x', 1, 2), ('d', 5, 1), ('y', 4, 2), ('y', 5, 2), ('x', 2, 2), ('d', 6, 1), ('y', 6, 2), ('y', 0, 3), ('y', 7, 2), ('x', 3, 2), ('y', 1, 3), ('x', 4, 2), ('y', 2, 3), ('x', 0, 3), ('y', 3, 3), ('y', 8, 2), ('y', 4, 3), ('x', 1, 3), ('y', 5, 3), ('x', 2, 3), ('d', 5, 2), ('y', 6, 3), ('y', 7, 3), ('d', 6, 2), ('x', 4, 3), ('x', 3, 3), ('y', 8, 3))


def kernel(
    in_hbm, val_hbm, gate_hbm, res_hbm, dec_hbm, skip_hbm, w_hbm, out_ref,
    res_ref, dec_ref, skip_ref, ig, vs, og, w2, px, py, prefix, states, g_out, g2, part,
    x_in, x_rel, x_drt, x_com, y_rel, y_drt, y_com, y_out, y_in, acc,
    load_sem, st_send, st_recv, pair_send, pair_recv, x_sem, y_sem,
):
    tokens, chans = px.shape[1], px.shape[0] * LANES
    steps = tokens // SUB
    modes = res_ref.shape[0]
    n_ctx = states.shape[0]
    groups = chans // LANES
    rows = out_ref.shape[0]
    wide = part.shape[3]

    ctx = lax.axis_index("ctx")
    tp = lax.axis_index("tp")
    core = lax.rem(tp, 2)
    y = lax.rem(lax.div(tp, 2), YS)
    xh = lax.div(tp, 2 * YS)

    def device(ctx_i, xh_i, y_i, core_i):
        return (ctx_i, (xh_i * YS + y_i) * 2 + core_i)

    partner = device(ctx, xh, y, 1 - core)
    up = device(ctx, xh, lax.rem(y + 1, YS), core)
    down = device(ctx, xh, lax.rem(y + YS - 1, YS), core)
    across = device(ctx, 1 - xh, y, core)
    far = device(ctx, xh, lax.rem(y + 2, YS), core)
    others = [(lax.rem(ctx + k, n_ctx), tp) for k in range(1, n_ctx)]

    barrier = pltpu.get_barrier_semaphore()
    peers = [partner, up, down, far, across] + others
    for peer in peers:
        pl.semaphore_signal(barrier, inc=1, device_id=peer, device_id_type=MESH)

    small = [
        pltpu.make_async_copy(dec_hbm, dec_ref, load_sem.at[4]),
        pltpu.make_async_copy(res_hbm, res_ref, load_sem.at[5]),
        pltpu.make_async_copy(skip_hbm, skip_ref, load_sem.at[6]),
    ]
    loads = [
        pltpu.make_async_copy(in_hbm, ig, load_sem.at[0]),
        pltpu.make_async_copy(val_hbm, vs, load_sem.at[1]),
        pltpu.make_async_copy(gate_hbm, og, load_sem.at[2]),
        pltpu.make_async_copy(w_hbm, w2.at[pl.ds(0, chans)], load_sem.at[3]),
    ]
    for load in loads[:2] + small + loads[2:]:
        load.start()
    loads[0].wait()
    loads[1].wait()

    for g in range(groups):
        lanes = pl.ds(g * LANES, LANES)
        product = (ig[:, lanes].astype(F32) * vs[:, lanes].astype(F32)).astype(BF16)
        px[g] = product.astype(F32)

    def spread(row):
        return jnp.broadcast_to(row, (SUB, LANES))

    position = lax.broadcasted_iota(jnp.int32, (SUB, LANES), 0)
    place = position.astype(F32)

    def group_decay(g):
        decay = dec_ref[:, pl.ds(g * LANES, LANES)]
        return decay, jnp.exp(-decay)

    for load in small:
        load.wait()

    for g in range(groups):
        lanes = pl.ds(g * LANES, LANES)
        decay, step_factor = group_decay(g)
        factors = [spread(step_factor[m : m + 1]) for m in range(modes)]

        def advance(i, held, factors=factors, g=g):
            x = px[g, pl.ds(i, SUB, stride=steps), :]
            return tuple(f * s + x for f, s in zip(factors, held))

        zero = jnp.zeros((SUB, LANES), F32)
        ends = lax.fori_loop(0, steps, advance, (zero,) * modes, unroll=8)
        for m in range(modes):
            rate = spread(decay[m : m + 1])
            tail = jnp.exp(-rate * ((SUB - 1 - place) * steps))
            states[ctx, m : m + 1, lanes] = jnp.sum(tail * ends[m], axis=0, keepdims=True)
            scan = jnp.where(position >= 1, pltpu.roll(ends[m], 1, 0), 0.0)
            for hop in (1, 2, 4):
                weight = jnp.where(position >= hop, jnp.exp(-rate * (hop * steps)), 0.0)
                scan = scan + weight * pltpu.roll(scan, hop, 0)
            prefix[g, m] = scan

    pl.semaphore_wait(barrier, len(peers))
    state_copies = []
    for k, peer in enumerate(others):
        copy = pltpu.make_async_remote_copy(
            src_ref=states.at[ctx], dst_ref=states.at[ctx],
            send_sem=st_send.at[k], recv_sem=st_recv.at[k],
            device_id=peer, device_id_type=MESH,
        )
        copy.start()
        state_copies.append(copy)
    w_copies = [
        pltpu.make_async_remote_copy(
            src_ref=w_hbm.at[pl.ds(h * chans // 2, chans // 2)],
            dst_ref=w2.at[pl.ds(chans + h * chans // 2, chans // 2)],
            send_sem=pair_send.at[groups + h], recv_sem=pair_recv.at[groups + h],
            device_id=partner, device_id_type=MESH,
        )
        for h in range(2)
    ]
    for copy in w_copies:
        copy.start()

    for g in range(groups):
        lanes = pl.ds(g * LANES, LANES)
        decay, step_factor = group_decay(g)
        amplitude = res_ref[:, lanes] * jnp.sqrt(2.0 * decay)
        factors = [spread(step_factor[m : m + 1]) for m in range(modes)]
        gains = [spread(amplitude[m : m + 1]) for m in range(modes)]

        def convolve(i, held, factors=factors, gains=gains, g=g):
            rows_i = pl.ds(i, SUB, stride=steps)
            x = px[g, rows_i, :]
            held = tuple(f * s + x for f, s in zip(factors, held))
            terms = [r * s for r, s in zip(gains, held)]
            while len(terms) > 1:
                terms = [terms[j] + terms[j + 1] for j in range(0, len(terms), 2)]
            py[g, rows_i, :] = terms[0]
            return held

        lax.fori_loop(0, steps, convolve, tuple(prefix[g, m] for m in range(modes)), unroll=4)

    for copy in state_copies:
        copy.wait_recv()

    loads[2].wait()

    def target_block(r, q, core_i):
        xh_t = lax.rem(xh + q, 2)
        return (xh_t * YS + lax.rem(y + r, YS)) * 2 + core_i

    def gated_rows(block, g):
        at = pl.ds(pl.multiple_of(block * rows, rows), rows)
        lanes = pl.ds(g * LANES, LANES)
        gate = og[at, lanes].astype(F32)
        return (gate * (py[g, at, :] + skip_ref[:, lanes] * px[g, at, :])).astype(BF16)

    g_copies = []
    for g in range(groups):
        lanes = pl.ds(g * LANES, LANES)
        decay, step_factor = group_decay(g)
        amplitude = res_ref[:, lanes] * jnp.sqrt(2.0 * decay)
        block_factor = jnp.exp(-decay * float(tokens))
        carried = jnp.zeros((modes, LANES), F32)
        for i in range(n_ctx - 1):
            carried = jnp.where(i < ctx, block_factor * carried + states[i, :, lanes], carried)
        carried = carried * amplitude
        factors = [spread(step_factor[m : m + 1]) for m in range(modes)]
        fades = tuple(
            spread(carried[m : m + 1]) * jnp.exp(-spread(decay[m : m + 1]) * (place * steps + 1.0))
            for m in range(modes)
        )

        def extend(i, fades, factors=factors, g=g):
            rows_i = pl.ds(i, SUB, stride=steps)
            terms = list(fades)
            while len(terms) > 1:
                terms = [terms[j] + terms[j + 1] for j in range(0, len(terms), 2)]
            py[g, rows_i, :] = py[g, rows_i, :] + terms[0]
            return tuple(f * v for f, v in zip(factors, fades))

        lax.fori_loop(0, steps, extend, fades, unroll=4)
        for r in range(YS):
            for q in range(2):
                g_out[g, pl.ds((q * YS + r) * rows, rows), :] = gated_rows(target_block(r, q, 1 - core), g)
        g_copy = pltpu.make_async_remote_copy(
            src_ref=g_out.at[g], dst_ref=g2.at[:, pl.ds(chans + g * LANES, LANES)],
            send_sem=pair_send.at[g], recv_sem=pair_recv.at[g],
            device_id=partner, device_id_type=MESH,
        )
        g_copy.start()
        g_copies.append(g_copy)
    for g in range(groups):
        for r in range(YS):
            for q in range(2):
                g2[pl.ds((q * YS + r) * rows, rows), pl.ds(g * LANES, LANES)] = gated_rows(
                    target_block(r, q, core), g
                )
    loads[3].wait()
    for copy in w_copies + g_copies:
        copy.wait_recv()

    half = YS * rows
    n_x, n_y = x_in.shape[0], y_in.shape[0]

    def send(src, dst, sems, k, to):
        return pltpu.make_async_remote_copy(
            src_ref=src, dst_ref=dst, send_sem=sems.at[0, k], recv_sem=sems.at[1, k],
            device_id=to, device_id_type=MESH,
        )

    def neighbour(turn):
        return device(ctx, xh, lax.rem(y + 1 + 2 * turn, YS), core)

    def block(r):
        return pl.ds(r * rows, rows)

    def y_first(k):
        turn = k % 2
        p = n_x + k
        src = part.at[p]
        return (
            p, 1 + 2 * turn,
            functools.partial(send, src.at[:, block(2)], y_rel.at[k], y_sem.at[0], k, neighbour(turn)),
            functools.partial(send, src.at[:, block(3 - 2 * turn)], y_drt.at[k], y_sem.at[1], k, neighbour(1 - turn)),
            functools.partial(send, src.at[:, block(1 + 2 * turn)], y_com.at[k], y_sem.at[2], k, neighbour(turn)),
            functools.partial(send, y_out.at[k], y_in.at[k], y_sem.at[3], k, across),
        )

    def x_first(k):
        turn = (k + 1) % 2
        src = part.at[k, 0]
        return (
            1 + 2 * turn,
            functools.partial(send, src.at[block(2)], x_rel.at[k], x_sem.at[0], k, neighbour(turn)),
            functools.partial(send, src.at[block(3 - 2 * turn)], x_drt.at[k], x_sem.at[1], k, neighbour(1 - turn)),
            functools.partial(send, src.at[block(1 + 2 * turn)], x_com.at[k], x_sem.at[2], k, neighbour(turn)),
            functools.partial(send, part.at[k, 1], x_in.at[k], x_sem.at[3], k, across),
        )

    def x_far(k):
        return send(part.at[k, 0, block(2)], x_rel.at[k], x_sem.at[0], k, far)

    def columns(p):
        return pl.ds(p * wide, wide)

    def multiply(p):
        product = jnp.dot(g2[...], w2[:, columns(p)], preferred_element_type=F32)
        part[p] = product.astype(BF16).reshape(2, half, wide)

    def x_start(k):
        multiply(k)
        x_first(k)[4]().start()

    def y_start(k):
        multiply(n_x + k)
        _, _, rel, drt, _, _ = y_first(k)
        rel().start()
        drt().start()


    def x_second(k):
        _, rel, drt, _, cross = x_first(k)
        cross().wait_recv()
        part[k, 0] = (part[k, 0].astype(F32) + x_in[k].astype(F32)).astype(BF16)
        rel().start()
        drt().start()

    def y_second(k):
        p, near, rel, _, com, _ = y_first(k)
        rel().wait_recv()
        part[p, :, block(near)] = (part[p, :, block(near)].astype(F32) + y_rel[k].astype(F32)).astype(BF16)
        com().start()


    def x_second_direct(k):
        _, _, drt, com, cross = x_first(k)
        cross().wait_recv()
        part[k, 0] = (part[k, 0].astype(F32) + x_in[k].astype(F32)).astype(BF16)
        x_far(k).start()
        drt().start()
        com().start()

    def x_last_direct(k):
        _, _, drt, com, cross = x_first(k)
        for copy in (x_far(k), drt(), com()):
            copy.wait_recv()
        summed = (
            part[k, 0, block(0)].astype(F32) + x_drt[k].astype(F32)
            + x_com[k].astype(F32) + x_rel[k].astype(F32)
        )
        out_ref[:, columns(k)] = summed.astype(BF16)
        for copy in (x_far(k), drt(), com(), cross()):
            copy.wait_send()

    def x_third(k):
        near, rel, _, com, _ = x_first(k)
        rel().wait_recv()
        part[k, 0, block(near)] = (part[k, 0, block(near)].astype(F32) + x_rel[k].astype(F32)).astype(BF16)
        com().start()

    def y_third(k):
        p, _, _, drt, com, cross = y_first(k)
        drt().wait_recv()
        com().wait_recv()
        summed = part[p, :, block(0)].astype(F32) + y_drt[k].astype(F32) + y_com[k].astype(F32)
        y_out[k] = summed[1].astype(BF16)
        cross().start()
        acc[k] = summed[0]


    def x_last(k):
        _, rel, drt, com, cross = x_first(k)
        drt().wait_recv()
        com().wait_recv()
        summed = part[k, 0, block(0)].astype(F32) + x_drt[k].astype(F32) + x_com[k].astype(F32)
        out_ref[:, columns(k)] = summed.astype(BF16)
        for copy in (rel, drt, com, cross):
            copy().wait_send()

    def y_last(k):
        p, _, rel, drt, com, cross = y_first(k)
        cross().wait_recv()
        out_ref[:, columns(p)] = (acc[k] + y_in[k].astype(F32)).astype(BF16)
        for copy in (rel, drt, com, cross):
            copy().wait_send()

    steps_of = {
        "x": (x_start, x_second, x_third, x_last),
        "d": (x_start, x_second_direct, x_last_direct),
        "y": (y_start, y_second, y_third, y_last),
    }
    for axis, k, stage in SCHEDULE:
        steps_of[axis][stage](k)
    for copy in state_copies + w_copies + g_copies:
        copy.wait_send()


def body(n_ctx, n_tp, in_gate, value_stream, out_gate, residues, decays, skip_gain, out_weight):
    tokens, chans = in_gate.shape
    modes = residues.shape[1]
    width = out_weight.shape[1]
    rows = tokens // n_tp
    wide = width // (X_PIECES + Y_PIECES)
    groups = chans // LANES
    hbm = pl.BlockSpec(memory_space=pltpu.HBM)
    vmem = pl.BlockSpec(memory_space=pltpu.VMEM)
    dma = pltpu.SemaphoreType.DMA
    return pl.pallas_call(
        kernel,
        out_shape=pltpu.VMEM((rows, width), BF16),
        in_specs=[hbm] * 7,
        out_specs=vmem,
        scratch_shapes=[
            pltpu.VMEM((modes, chans), F32),
            pltpu.VMEM((modes, chans), F32),
            pltpu.VMEM((1, chans), F32),
            pltpu.VMEM((tokens, chans), BF16),
            pltpu.VMEM((tokens, chans), BF16),
            pltpu.VMEM((tokens, chans), BF16),
            pltpu.VMEM((2 * chans, width), BF16),
            pltpu.VMEM((groups, tokens, LANES), F32),
            pltpu.VMEM((groups, tokens, LANES), F32),
            pltpu.VMEM((groups, modes, SUB, LANES), F32),
            pltpu.VMEM((n_ctx, modes, chans), F32),
            pltpu.VMEM((groups, tokens // 2, LANES), BF16),
            pltpu.VMEM((tokens // 2, 2 * chans), BF16),
            pltpu.VMEM((X_PIECES + Y_PIECES, 2, YS * rows, wide), BF16),
            pltpu.VMEM((X_PIECES, YS * rows, wide), BF16),
            pltpu.VMEM((X_PIECES, rows, wide), BF16),
            pltpu.VMEM((X_PIECES, rows, wide), BF16),
            pltpu.VMEM((X_PIECES, rows, wide), BF16),
            pltpu.VMEM((Y_PIECES, 2, rows, wide), BF16),
            pltpu.VMEM((Y_PIECES, 2, rows, wide), BF16),
            pltpu.VMEM((Y_PIECES, 2, rows, wide), BF16),
            pltpu.VMEM((Y_PIECES, rows, wide), BF16),
            pltpu.VMEM((Y_PIECES, rows, wide), BF16),
            pltpu.VMEM((Y_PIECES, rows, wide), F32),
            dma((7,)),
            dma((n_ctx - 1,)),
            dma((n_ctx - 1,)),
            dma((groups + 2,)),
            dma((groups + 2,)),
            dma((4, 2, X_PIECES)),
            dma((4, 2, Y_PIECES)),
        ],
        compiler_params=pltpu.CompilerParams(
            collective_id=0, has_side_effects=True, vmem_limit_bytes=48 * 1024 * 1024
        ),
        cost_estimate=pl.CostEstimate(
            flops=2 * tokens * chans * width, bytes_accessed=4 * 1024 * 1024, transcendentals=0
        ),
    )(
        *(
            pltpu.with_memory_space_constraint(operand, pltpu.HBM)
            for operand in (
                in_gate, value_stream, out_gate, residues.T, decays.T, skip_gain.reshape(1, chans), out_weight
            )
        )
    )


def solution(mesh):
    n_ctx, n_tp = mesh.shape["ctx"], mesh.shape["tp"]
    in_specs = (
        P("ctx", "tp"),
        P("ctx", "tp"),
        P("ctx", "tp"),
        P("tp", None),
        P("tp", None),
        P("tp"),
        P("tp", None),
    )
    out_specs = P(("ctx", "tp"), None)
    return jax.shard_map(
        functools.partial(body, n_ctx, n_tp),
        mesh=mesh, in_specs=in_specs, out_specs=out_specs, check_vma=False,
    )
```

```python
import functools

import jax
import jax.numpy as jnp
from jax import lax
from jax.experimental import pallas as pl
from jax.experimental.pallas import tpu as pltpu
from jax.sharding import PartitionSpec as P

MESH = pl.DeviceIdType.MESH
F32 = jnp.float32
BF16 = jnp.bfloat16

LANES = 128
SUB = 8
YS = 4
X_PIECES, Y_PIECES = 7, 9

SCHEDULE = (('y', 0, 0), ('x', 0, 0), ('y', 1, 0), ('x', 1, 0), ('y', 2, 0), ('x', 2, 0), ('y', 3, 0), ('x', 3, 0), ('y', 4, 0), ('x', 4, 0), ('y', 5, 0), ('d', 5, 0), ('y', 6, 0), ('d', 6, 0), ('y', 7, 0), ('y', 8, 0), ('y', 0, 1), ('y', 1, 1), ('x', 0, 1), ('y', 2, 1), ('y', 3, 1), ('x', 1, 1), ('y', 4, 1), ('y', 5, 1), ('x', 2, 1), ('y', 6, 1), ('y', 7, 1), ('x', 3, 1), ('y', 8, 1), ('y', 0, 2), ('x', 4, 1), ('y', 1, 2), ('x', 0, 2), ('y', 2, 2), ('y', 3, 2), ('x', 1, 2), ('d', 5, 1), ('y', 4, 2), ('y', 5, 2), ('x', 2, 2), ('d', 6, 1), ('y', 6, 2), ('y', 0, 3), ('y', 7, 2), ('x', 3, 2), ('y', 1, 3), ('x', 4, 2), ('y', 2, 3), ('x', 0, 3), ('y', 3, 3), ('y', 8, 2), ('y', 4, 3), ('x', 1, 3), ('y', 5, 3), ('x', 2, 3), ('d', 5, 2), ('y', 6, 3), ('y', 7, 3), ('d', 6, 2), ('x', 4, 3), ('x', 3, 3), ('y', 8, 3))


def kernel(
    in_hbm, val_hbm, gate_hbm, res_hbm, dec_hbm, skip_hbm, w_hbm, out_ref,
    res_ref, dec_ref, skip_ref, ig, vs, og, w2, px, py, prefix, states, g_out, g2, part,
    x_in, x_rel, x_drt, x_com, y_rel, y_drt, y_com, y_out, y_in, acc,
    load_sem, st_send, st_recv, pair_send, pair_recv, x_sem, y_sem,
):
    tokens, chans = px.shape[1], px.shape[0] * LANES
    steps = tokens // SUB
    modes = res_ref.shape[0]
    n_ctx = states.shape[0]
    groups = chans // LANES
    rows = out_ref.shape[0]
    wide = part.shape[3]

    ctx = lax.axis_index("ctx")
    tp = lax.axis_index("tp")
    core = lax.rem(tp, 2)
    y = lax.rem(lax.div(tp, 2), YS)
    xh = lax.div(tp, 2 * YS)

    def device(ctx_i, xh_i, y_i, core_i):
        return (ctx_i, (xh_i * YS + y_i) * 2 + core_i)

    partner = device(ctx, xh, y, 1 - core)
    up = device(ctx, xh, lax.rem(y + 1, YS), core)
    down = device(ctx, xh, lax.rem(y + YS - 1, YS), core)
    across = device(ctx, 1 - xh, y, core)
    far = device(ctx, xh, lax.rem(y + 2, YS), core)

    small = [
        pltpu.make_async_copy(dec_hbm, dec_ref, load_sem.at[4]),
        pltpu.make_async_copy(res_hbm, res_ref, load_sem.at[5]),
        pltpu.make_async_copy(skip_hbm, skip_ref, load_sem.at[6]),
    ]
    loads = [
        pltpu.make_async_copy(in_hbm, ig, load_sem.at[0]),
        pltpu.make_async_copy(val_hbm, vs, load_sem.at[1]),
        pltpu.make_async_copy(gate_hbm, og, load_sem.at[2]),
        pltpu.make_async_copy(w_hbm, w2.at[pl.ds(0, chans)], load_sem.at[3]),
    ]
    for load in loads[:2] + small:
        load.start()
    barrier = pltpu.get_barrier_semaphore()
    peers = [partner, up, down, far, across]
    for peer in peers:
        pl.semaphore_signal(barrier, inc=1, device_id=peer, device_id_type=MESH)
    for k in range(1, n_ctx):

        @pl.when(ctx >= k)
        def _(k=k):
            pl.semaphore_signal(barrier, inc=1, device_id=(ctx - k, tp), device_id_type=MESH)

    loads[0].wait()
    loads[1].wait()
    for load in loads[2:]:
        load.start()

    for g in range(groups):
        lanes = pl.ds(g * LANES, LANES)
        product = (ig[:, lanes].astype(F32) * vs[:, lanes].astype(F32)).astype(BF16)
        px[g] = product.astype(F32)

    def spread(row):
        return jnp.broadcast_to(row, (SUB, LANES))

    position = lax.broadcasted_iota(jnp.int32, (SUB, LANES), 0)
    place = position.astype(F32)

    def group_decay(g):
        decay = dec_ref[:, pl.ds(g * LANES, LANES)]
        return decay, jnp.exp(-decay)

    for load in small:
        load.wait()

    for g in range(groups):
        lanes = pl.ds(g * LANES, LANES)
        decay, step_factor = group_decay(g)
        factors = [spread(step_factor[m : m + 1]) for m in range(modes)]

        def advance(i, held, factors=factors, g=g):
            x = px[g, pl.ds(i, SUB, stride=steps), :]
            return tuple(f * s + x for f, s in zip(factors, held))

        zero = jnp.zeros((SUB, LANES), F32)
        ends = lax.fori_loop(0, steps, advance, (zero,) * modes, unroll=8)
        for m in range(modes):
            rate = spread(decay[m : m + 1])
            tail = jnp.exp(-rate * ((SUB - 1 - place) * steps))
            states[ctx, m : m + 1, lanes] = jnp.sum(tail * ends[m], axis=0, keepdims=True)
            scan = jnp.where(position >= 1, pltpu.roll(ends[m], 1, 0), 0.0)
            for hop in (1, 2, 4):
                weight = jnp.where(position >= hop, jnp.exp(-rate * (hop * steps)), 0.0)
                scan = scan + weight * pltpu.roll(scan, hop, 0)
            prefix[g, m] = scan

    pl.semaphore_wait(barrier, len(peers) + n_ctx - 1 - ctx)

    def state_copy(k):
        return pltpu.make_async_remote_copy(
            src_ref=states.at[ctx], dst_ref=states.at[ctx],
            send_sem=st_send.at[k - 1], recv_sem=st_recv.at[k - 1],
            device_id=(lax.rem(ctx + k, n_ctx), tp), device_id_type=MESH,
        )

    for k in range(1, n_ctx):

        @pl.when(ctx + k < n_ctx)
        def _(k=k):
            state_copy(k).start()

    w_copies = [
        pltpu.make_async_remote_copy(
            src_ref=w_hbm.at[pl.ds(h * chans // 2, chans // 2)],
            dst_ref=w2.at[pl.ds(chans + h * chans // 2, chans // 2)],
            send_sem=pair_send.at[groups + h], recv_sem=pair_recv.at[groups + h],
            device_id=partner, device_id_type=MESH,
        )
        for h in range(2)
    ]
    for copy in w_copies:
        copy.start()

    for g in range(groups):
        lanes = pl.ds(g * LANES, LANES)
        decay, step_factor = group_decay(g)
        amplitude = res_ref[:, lanes] * jnp.sqrt(2.0 * decay)
        factors = [spread(step_factor[m : m + 1]) for m in range(modes)]
        gains = [spread(amplitude[m : m + 1]) for m in range(modes)]

        def convolve(i, held, factors=factors, gains=gains, g=g):
            rows_i = pl.ds(i, SUB, stride=steps)
            x = px[g, rows_i, :]
            held = tuple(f * s + x for f, s in zip(factors, held))
            terms = [r * s for r, s in zip(gains, held)]
            while len(terms) > 1:
                terms = [terms[j] + terms[j + 1] for j in range(0, len(terms), 2)]
            py[g, rows_i, :] = terms[0]
            return held

        lax.fori_loop(0, steps, convolve, tuple(prefix[g, m] for m in range(modes)), unroll=4)

    for k in range(1, n_ctx):

        @pl.when(ctx >= k)
        def _(k=k):
            state_copy(k).wait_recv()


    loads[2].wait()

    def target_block(r, q, core_i):
        xh_t = lax.rem(xh + q, 2)
        return (xh_t * YS + lax.rem(y + r, YS)) * 2 + core_i

    def gated_rows(block, g):
        at = pl.ds(pl.multiple_of(block * rows, rows), rows)
        lanes = pl.ds(g * LANES, LANES)
        gate = og[at, lanes].astype(F32)
        return (gate * (py[g, at, :] + skip_ref[:, lanes] * px[g, at, :])).astype(BF16)

    def carry_in(g):
        lanes = pl.ds(g * LANES, LANES)
        decay, step_factor = group_decay(g)
        amplitude = res_ref[:, lanes] * jnp.sqrt(2.0 * decay)
        block_factor = jnp.exp(-decay * float(tokens))

        def collect(i, carried):
            return block_factor * carried + states[i, :, lanes]

        return lax.fori_loop(0, ctx, collect, jnp.zeros((modes, LANES), F32)) * amplitude

    def extend_rows(g, carried, owner):
        decay, step_factor = group_decay(g)
        first = owner * rows
        factors = [spread(step_factor[m : m + 1]) for m in range(modes)]
        ahead = place * steps + (first + 1).astype(F32)
        fades = tuple(
            spread(carried[m : m + 1]) * jnp.exp(-spread(decay[m : m + 1]) * ahead) for m in range(modes)
        )

        def extend(i, fades):
            rows_i = pl.ds(first + i, SUB, stride=steps)
            terms = list(fades)
            while len(terms) > 1:
                terms = [terms[j] + terms[j + 1] for j in range(0, len(terms), 2)]
            py[g, rows_i, :] = py[g, rows_i, :] + terms[0]
            return tuple(f * v for f, v in zip(factors, fades))

        lax.fori_loop(0, rows, extend, fades, unroll=4)

    g_copies = []
    carries = []
    for g in range(groups):
        carries.append(carry_in(g))
        extend_rows(g, carries[g], 1 - core)
        for r in range(YS):
            for q in range(2):
                g_out[g, pl.ds((q * YS + r) * rows, rows), :] = gated_rows(target_block(r, q, 1 - core), g)
        g_copy = pltpu.make_async_remote_copy(
            src_ref=g_out.at[g], dst_ref=g2.at[:, pl.ds(chans + g * LANES, LANES)],
            send_sem=pair_send.at[g], recv_sem=pair_recv.at[g],
            device_id=partner, device_id_type=MESH,
        )
        g_copy.start()
        g_copies.append(g_copy)
    for g in range(groups):
        extend_rows(g, carries[g], core)
        for r in range(YS):
            for q in range(2):
                g2[pl.ds((q * YS + r) * rows, rows), pl.ds(g * LANES, LANES)] = gated_rows(
                    target_block(r, q, core), g
                )
    loads[3].wait()
    for copy in w_copies + g_copies:
        copy.wait_recv()

    half = YS * rows
    n_x, n_y = x_in.shape[0], y_in.shape[0]

    def send(src, dst, sems, k, to):
        return pltpu.make_async_remote_copy(
            src_ref=src, dst_ref=dst, send_sem=sems.at[0, k], recv_sem=sems.at[1, k],
            device_id=to, device_id_type=MESH,
        )

    def neighbour(turn):
        return device(ctx, xh, lax.rem(y + 1 + 2 * turn, YS), core)

    def block(r):
        return pl.ds(r * rows, rows)

    def y_first(k):
        turn = k % 2
        p = n_x + k
        src = part.at[p]
        return (
            p, 1 + 2 * turn,
            functools.partial(send, src.at[:, block(2)], y_rel.at[k], y_sem.at[0], k, neighbour(turn)),
            functools.partial(send, src.at[:, block(3 - 2 * turn)], y_drt.at[k], y_sem.at[1], k, neighbour(1 - turn)),
            functools.partial(send, src.at[:, block(1 + 2 * turn)], y_com.at[k], y_sem.at[2], k, neighbour(turn)),
            functools.partial(send, y_out.at[k], y_in.at[k], y_sem.at[3], k, across),
        )

    def x_first(k):
        turn = (k + 1) % 2
        src = part.at[k, 0]
        return (
            1 + 2 * turn,
            functools.partial(send, src.at[block(2)], x_rel.at[k], x_sem.at[0], k, neighbour(turn)),
            functools.partial(send, src.at[block(3 - 2 * turn)], x_drt.at[k], x_sem.at[1], k, neighbour(1 - turn)),
            functools.partial(send, src.at[block(1 + 2 * turn)], x_com.at[k], x_sem.at[2], k, neighbour(turn)),
            functools.partial(send, part.at[k, 1], x_in.at[k], x_sem.at[3], k, across),
        )

    def x_far(k):
        return send(part.at[k, 0, block(2)], x_rel.at[k], x_sem.at[0], k, far)

    def columns(p):
        return pl.ds(p * wide, wide)

    def multiply(p):
        product = jnp.dot(g2[...], w2[:, columns(p)], preferred_element_type=F32)
        part[p] = product.astype(BF16).reshape(2, half, wide)

    def x_start(k):
        multiply(k)
        x_first(k)[4]().start()

    def y_start(k):
        multiply(n_x + k)
        _, _, rel, drt, _, _ = y_first(k)
        rel().start()
        drt().start()


    def x_second(k):
        _, rel, drt, _, cross = x_first(k)
        cross().wait_recv()
        part[k, 0] = (part[k, 0].astype(F32) + x_in[k].astype(F32)).astype(BF16)
        rel().start()
        drt().start()

    def y_second(k):
        p, near, rel, _, com, _ = y_first(k)
        rel().wait_recv()
        part[p, :, block(near)] = (part[p, :, block(near)].astype(F32) + y_rel[k].astype(F32)).astype(BF16)
        com().start()


    def x_second_direct(k):
        _, _, drt, com, cross = x_first(k)
        cross().wait_recv()
        part[k, 0] = (part[k, 0].astype(F32) + x_in[k].astype(F32)).astype(BF16)
        x_far(k).start()
        drt().start()
        com().start()

    def x_last_direct(k):
        _, _, drt, com, cross = x_first(k)
        for copy in (x_far(k), drt(), com()):
            copy.wait_recv()
        summed = (
            part[k, 0, block(0)].astype(F32) + x_drt[k].astype(F32)
            + x_com[k].astype(F32) + x_rel[k].astype(F32)
        )
        out_ref[:, columns(k)] = summed.astype(BF16)
        for copy in (x_far(k), drt(), com(), cross()):
            copy.wait_send()

    def x_third(k):
        near, rel, _, com, _ = x_first(k)
        rel().wait_recv()
        part[k, 0, block(near)] = (part[k, 0, block(near)].astype(F32) + x_rel[k].astype(F32)).astype(BF16)
        com().start()

    def y_third(k):
        p, _, _, drt, com, cross = y_first(k)
        drt().wait_recv()
        com().wait_recv()
        summed = part[p, :, block(0)].astype(F32) + y_drt[k].astype(F32) + y_com[k].astype(F32)
        y_out[k] = summed[1].astype(BF16)
        cross().start()
        acc[k] = summed[0]


    def x_last(k):
        _, rel, drt, com, cross = x_first(k)
        drt().wait_recv()
        com().wait_recv()
        summed = part[k, 0, block(0)].astype(F32) + x_drt[k].astype(F32) + x_com[k].astype(F32)
        out_ref[:, columns(k)] = summed.astype(BF16)
        for copy in (rel, drt, com, cross):
            copy().wait_send()

    def y_last(k):
        p, _, rel, drt, com, cross = y_first(k)
        cross().wait_recv()
        out_ref[:, columns(p)] = (acc[k] + y_in[k].astype(F32)).astype(BF16)
        for copy in (rel, drt, com, cross):
            copy().wait_send()

    steps_of = {
        "x": (x_start, x_second, x_third, x_last),
        "d": (x_start, x_second_direct, x_last_direct),
        "y": (y_start, y_second, y_third, y_last),
    }
    for axis, k, stage in SCHEDULE:
        steps_of[axis][stage](k)
    for k in range(1, n_ctx):

        @pl.when(ctx + k < n_ctx)
        def _(k=k):
            state_copy(k).wait_send()

    for copy in w_copies + g_copies:
        copy.wait_send()


def body(n_ctx, n_tp, in_gate, value_stream, out_gate, residues, decays, skip_gain, out_weight):
    tokens, chans = in_gate.shape
    modes = residues.shape[1]
    width = out_weight.shape[1]
    rows = tokens // n_tp
    wide = width // (X_PIECES + Y_PIECES)
    groups = chans // LANES
    hbm = pl.BlockSpec(memory_space=pltpu.HBM)
    vmem = pl.BlockSpec(memory_space=pltpu.VMEM)
    dma = pltpu.SemaphoreType.DMA
    return pl.pallas_call(
        kernel,
        out_shape=pltpu.VMEM((rows, width), BF16),
        in_specs=[hbm] * 7,
        out_specs=vmem,
        scratch_shapes=[
            pltpu.VMEM((modes, chans), F32),
            pltpu.VMEM((modes, chans), F32),
            pltpu.VMEM((1, chans), F32),
            pltpu.VMEM((tokens, chans), BF16),
            pltpu.VMEM((tokens, chans), BF16),
            pltpu.VMEM((tokens, chans), BF16),
            pltpu.VMEM((2 * chans, width), BF16),
            pltpu.VMEM((groups, tokens, LANES), F32),
            pltpu.VMEM((groups, tokens, LANES), F32),
            pltpu.VMEM((groups, modes, SUB, LANES), F32),
            pltpu.VMEM((n_ctx, modes, chans), F32),
            pltpu.VMEM((groups, tokens // 2, LANES), BF16),
            pltpu.VMEM((tokens // 2, 2 * chans), BF16),
            pltpu.VMEM((X_PIECES + Y_PIECES, 2, YS * rows, wide), BF16),
            pltpu.VMEM((X_PIECES, YS * rows, wide), BF16),
            pltpu.VMEM((X_PIECES, rows, wide), BF16),
            pltpu.VMEM((X_PIECES, rows, wide), BF16),
            pltpu.VMEM((X_PIECES, rows, wide), BF16),
            pltpu.VMEM((Y_PIECES, 2, rows, wide), BF16),
            pltpu.VMEM((Y_PIECES, 2, rows, wide), BF16),
            pltpu.VMEM((Y_PIECES, 2, rows, wide), BF16),
            pltpu.VMEM((Y_PIECES, rows, wide), BF16),
            pltpu.VMEM((Y_PIECES, rows, wide), BF16),
            pltpu.VMEM((Y_PIECES, rows, wide), F32),
            dma((7,)),
            dma((n_ctx - 1,)),
            dma((n_ctx - 1,)),
            dma((groups + 2,)),
            dma((groups + 2,)),
            dma((4, 2, X_PIECES)),
            dma((4, 2, Y_PIECES)),
        ],
        compiler_params=pltpu.CompilerParams(
            collective_id=0, has_side_effects=True, vmem_limit_bytes=48 * 1024 * 1024
        ),
        cost_estimate=pl.CostEstimate(
            flops=2 * tokens * chans * width, bytes_accessed=4 * 1024 * 1024, transcendentals=0
        ),
    )(
        *(
            pltpu.with_memory_space_constraint(operand, pltpu.HBM)
            for operand in (
                in_gate, value_stream, out_gate, residues.T, decays.T, skip_gain.reshape(1, chans), out_weight
            )
        )
    )


def solution(mesh):
    n_ctx, n_tp = mesh.shape["ctx"], mesh.shape["tp"]
    in_specs = (
        P("ctx", "tp"),
        P("ctx", "tp"),
        P("ctx", "tp"),
        P("tp", None),
        P("tp", None),
        P("tp"),
        P("tp", None),
    )
    out_specs = P(("ctx", "tp"), None)
    return jax.shard_map(
        functools.partial(body, n_ctx, n_tp),
        mesh=mesh, in_specs=in_specs, out_specs=out_specs, check_vma=False,
    )
```

```python
import functools

import jax
import jax.numpy as jnp
from jax import lax
from jax.experimental import pallas as pl
from jax.experimental.pallas import tpu as pltpu
from jax.sharding import PartitionSpec as P

MESH = pl.DeviceIdType.MESH
F32 = jnp.float32
BF16 = jnp.bfloat16

LANES = 128
SUB = 8
YS = 4
W_CHUNKS = 4
X_PIECES, Y_PIECES = 7, 9

SCHEDULE = (('y', 0, 0), ('x', 0, 0), ('y', 1, 0), ('x', 1, 0), ('y', 2, 0), ('x', 2, 0), ('y', 3, 0), ('x', 3, 0), ('y', 4, 0), ('x', 4, 0), ('y', 5, 0), ('d', 5, 0), ('y', 6, 0), ('d', 6, 0), ('y', 7, 0), ('y', 8, 0), ('y', 0, 1), ('y', 1, 1), ('x', 0, 1), ('y', 2, 1), ('y', 3, 1), ('x', 1, 1), ('y', 4, 1), ('y', 5, 1), ('x', 2, 1), ('y', 6, 1), ('y', 7, 1), ('x', 3, 1), ('y', 8, 1), ('y', 0, 2), ('x', 4, 1), ('y', 1, 2), ('x', 0, 2), ('y', 2, 2), ('y', 3, 2), ('x', 1, 2), ('d', 5, 1), ('y', 4, 2), ('y', 5, 2), ('x', 2, 2), ('d', 6, 1), ('y', 6, 2), ('y', 0, 3), ('y', 7, 2), ('x', 3, 2), ('y', 1, 3), ('x', 4, 2), ('y', 2, 3), ('x', 0, 3), ('y', 3, 3), ('y', 8, 2), ('y', 4, 3), ('x', 1, 3), ('y', 5, 3), ('x', 2, 3), ('d', 5, 2), ('y', 6, 3), ('y', 7, 3), ('d', 6, 2), ('x', 4, 3), ('x', 3, 3), ('y', 8, 3))


def kernel(
    in_hbm, val_hbm, gate_hbm, res_hbm, dec_hbm, skip_hbm, w_hbm, out_ref,
    res_ref, dec_ref, skip_ref, ig, vs, og, w2, px, py, prefix, states, g_out, g2, part,
    x_in, x_rel, x_dc, y_rel, y_dc, y_out, y_in, acc,
    load_sem, st_send, st_recv, pair_send, pair_recv, sent, x_sem, y_sem,
):
    tokens, chans = px.shape[1], px.shape[0] * LANES
    steps = tokens // SUB
    modes = res_ref.shape[0]
    n_ctx = states.shape[0]
    groups = chans // LANES
    rows = out_ref.shape[0]
    wide = part.shape[3]

    ctx = lax.axis_index("ctx")
    tp = lax.axis_index("tp")
    core = lax.rem(tp, 2)
    y = lax.rem(lax.div(tp, 2), YS)
    xh = lax.div(tp, 2 * YS)

    def device(ctx_i, xh_i, y_i, core_i):
        return (ctx_i, (xh_i * YS + y_i) * 2 + core_i)

    partner = device(ctx, xh, y, 1 - core)
    up = device(ctx, xh, lax.rem(y + 1, YS), core)
    down = device(ctx, xh, lax.rem(y + YS - 1, YS), core)
    across = device(ctx, 1 - xh, y, core)
    far = device(ctx, xh, lax.rem(y + 2, YS), core)

    small = [
        pltpu.make_async_copy(dec_hbm, dec_ref, load_sem.at[4]),
        pltpu.make_async_copy(res_hbm, res_ref, load_sem.at[5]),
        pltpu.make_async_copy(skip_hbm, skip_ref, load_sem.at[6]),
    ]
    loads = [
        pltpu.make_async_copy(in_hbm, ig, load_sem.at[0]),
        pltpu.make_async_copy(val_hbm, vs, load_sem.at[1]),
        pltpu.make_async_copy(gate_hbm, og, load_sem.at[2]),
        pltpu.make_async_copy(w_hbm, w2.at[pl.ds(0, chans)], load_sem.at[3]),
    ]
    for load in loads[:2] + small:
        load.start()
    barrier = pltpu.get_barrier_semaphore()
    peers = [partner, up, down, far, across]
    for peer in peers:
        pl.semaphore_signal(barrier, inc=1, device_id=peer, device_id_type=MESH)
    for k in range(1, n_ctx):

        @pl.when(ctx >= k)
        def _(k=k):
            pl.semaphore_signal(barrier, inc=1, device_id=(ctx - k, tp), device_id_type=MESH)

    loads[0].wait()
    loads[1].wait()
    for load in loads[2:]:
        load.start()

    for g in range(groups):
        lanes = pl.ds(g * LANES, LANES)
        product = (ig[:, lanes].astype(F32) * vs[:, lanes].astype(F32)).astype(BF16)
        px[g] = product.astype(F32)

    def spread(row):
        return jnp.broadcast_to(row, (SUB, LANES))

    position = lax.broadcasted_iota(jnp.int32, (SUB, LANES), 0)
    place = position.astype(F32)

    def group_decay(g):
        decay = dec_ref[:, pl.ds(g * LANES, LANES)]
        return decay, jnp.exp(-decay)

    for load in small:
        load.wait()

    for g in range(groups):
        lanes = pl.ds(g * LANES, LANES)
        decay, step_factor = group_decay(g)
        factors = [spread(step_factor[m : m + 1]) for m in range(modes)]

        def advance(i, held, factors=factors, g=g):
            x = px[g, pl.ds(i, SUB, stride=steps), :]
            return tuple(f * s + x for f, s in zip(factors, held))

        zero = jnp.zeros((SUB, LANES), F32)
        ends = lax.fori_loop(0, steps, advance, (zero,) * modes, unroll=8)
        for m in range(modes):
            rate = spread(decay[m : m + 1])
            tail = jnp.exp(-rate * ((SUB - 1 - place) * steps))
            states[ctx, m : m + 1, lanes] = jnp.sum(tail * ends[m], axis=0, keepdims=True)
            scan = jnp.where(position >= 1, pltpu.roll(ends[m], 1, 0), 0.0)
            for hop in (1, 2, 4):
                weight = jnp.where(position >= hop, jnp.exp(-rate * (hop * steps)), 0.0)
                scan = scan + weight * pltpu.roll(scan, hop, 0)
            prefix[g, m] = scan

    pl.semaphore_wait(barrier, len(peers) + n_ctx - 1 - ctx)

    def state_copy(k):
        return pltpu.make_async_remote_copy(
            src_ref=states.at[ctx], dst_ref=states.at[ctx],
            send_sem=st_send.at[k - 1], recv_sem=st_recv.at[k - 1],
            device_id=(lax.rem(ctx + k, n_ctx), tp), device_id_type=MESH,
        )

    for k in range(1, n_ctx):

        @pl.when(ctx + k < n_ctx)
        def _(k=k):
            state_copy(k).start()

    chunk = w2.shape[1] // W_CHUNKS
    w_copies = [
        pltpu.make_async_remote_copy(
            src_ref=w_hbm.at[:, pl.ds(c * chunk, chunk)],
            dst_ref=w2.at[pl.ds(chans, chans), pl.ds(c * chunk, chunk)],
            send_sem=pair_send.at[groups + c], recv_sem=pair_recv.at[groups + c],
            device_id=partner, device_id_type=MESH,
        )
        for c in range(W_CHUNKS)
    ]
    for copy in w_copies[: W_CHUNKS // 2]:
        copy.start()

    for g in range(groups):
        lanes = pl.ds(g * LANES, LANES)
        decay, step_factor = group_decay(g)
        amplitude = res_ref[:, lanes] * jnp.sqrt(2.0 * decay)
        factors = [spread(step_factor[m : m + 1]) for m in range(modes)]
        gains = [spread(amplitude[m : m + 1]) for m in range(modes)]

        def convolve(i, held, factors=factors, gains=gains, g=g):
            rows_i = pl.ds(i, SUB, stride=steps)
            x = px[g, rows_i, :]
            held = tuple(f * s + x for f, s in zip(factors, held))
            terms = [r * s for r, s in zip(gains, held)]
            while len(terms) > 1:
                terms = [terms[j] + terms[j + 1] for j in range(0, len(terms), 2)]
            py[g, rows_i, :] = terms[0]
            return held

        lax.fori_loop(0, steps, convolve, tuple(prefix[g, m] for m in range(modes)), unroll=4)

    for k in range(1, n_ctx):

        @pl.when(ctx >= k)
        def _(k=k):
            state_copy(k).wait_recv()


    loads[2].wait()

    def target_block(r, q, core_i):
        xh_t = lax.rem(xh + q, 2)
        return (xh_t * YS + lax.rem(y + r, YS)) * 2 + core_i

    def gated_rows(block, g):
        at = pl.ds(pl.multiple_of(block * rows, rows), rows)
        lanes = pl.ds(g * LANES, LANES)
        gate = og[at, lanes].astype(F32)
        return (gate * (py[g, at, :] + skip_ref[:, lanes] * px[g, at, :])).astype(BF16)

    def carry_in(g):
        lanes = pl.ds(g * LANES, LANES)
        decay, step_factor = group_decay(g)
        amplitude = res_ref[:, lanes] * jnp.sqrt(2.0 * decay)
        block_factor = jnp.exp(-decay * float(tokens))

        def collect(i, carried):
            return block_factor * carried + states[i, :, lanes]

        return lax.fori_loop(0, ctx, collect, jnp.zeros((modes, LANES), F32)) * amplitude

    def extend_rows(g, carried, owner):
        decay, step_factor = group_decay(g)
        first = owner * rows
        factors = [spread(step_factor[m : m + 1]) for m in range(modes)]
        ahead = place * steps + (first + 1).astype(F32)
        fades = tuple(
            spread(carried[m : m + 1]) * jnp.exp(-spread(decay[m : m + 1]) * ahead) for m in range(modes)
        )

        def extend(i, fades):
            rows_i = pl.ds(first + i, SUB, stride=steps)
            terms = list(fades)
            while len(terms) > 1:
                terms = [terms[j] + terms[j + 1] for j in range(0, len(terms), 2)]
            py[g, rows_i, :] = py[g, rows_i, :] + terms[0]
            return tuple(f * v for f, v in zip(factors, fades))

        lax.fori_loop(0, rows, extend, fades, unroll=4)

    g_copies = []
    carries = []
    for g in range(groups):
        carries.append(carry_in(g))
        extend_rows(g, carries[g], 1 - core)
        for r in range(YS):
            for q in range(2):
                g_out[g, pl.ds((q * YS + r) * rows, rows), :] = gated_rows(target_block(r, q, 1 - core), g)
        g_copy = pltpu.make_async_remote_copy(
            src_ref=g_out.at[g], dst_ref=g2.at[:, pl.ds(chans + g * LANES, LANES)],
            send_sem=pair_send.at[g], recv_sem=pair_recv.at[g],
            device_id=partner, device_id_type=MESH,
        )
        g_copy.start()
        g_copies.append(g_copy)
    for copy in w_copies[W_CHUNKS // 2 :]:
        copy.start()
    for g in range(groups):
        extend_rows(g, carries[g], core)
        for r in range(YS):
            for q in range(2):
                g2[pl.ds((q * YS + r) * rows, rows), pl.ds(g * LANES, LANES)] = gated_rows(
                    target_block(r, q, core), g
                )
    loads[3].wait()
    for copy in g_copies:
        copy.wait_recv()

    half = YS * rows
    n_x, n_y = x_in.shape[0], y_in.shape[0]

    def send(src, dst, kind, sem, to):
        return pltpu.make_async_remote_copy(
            src_ref=src, dst_ref=dst, send_sem=sent.at[kind], recv_sem=sem,
            device_id=to, device_id_type=MESH,
        )

    def landed(dst, sem):
        send(dst, dst, 0, sem, across).wait_recv()

    def neighbour(turn):
        return device(ctx, xh, lax.rem(y + 1 + 2 * turn, YS), core)

    def block(r):
        return pl.ds(r * rows, rows)

    def y_first(k):
        turn = k % 2
        p = n_x + k
        src = part.at[p]
        return (
            p, 1 + 2 * turn,
            functools.partial(send, src.at[:, block(2)], y_rel.at[k], 0, y_sem.at[0, k], neighbour(turn)),
            functools.partial(send, src.at[:, block(3 - 2 * turn)], y_dc.at[k, 0], 1, y_sem.at[1, k], neighbour(1 - turn)),
            functools.partial(send, src.at[:, block(1 + 2 * turn)], y_dc.at[k, 1], 1, y_sem.at[1, k], neighbour(turn)),
            functools.partial(send, y_out.at[k], y_in.at[k], 2, y_sem.at[2, k], across),
        )

    def x_first(k):
        turn = (k + 1) % 2
        src = part.at[k, 0]
        return (
            1 + 2 * turn,
            functools.partial(send, src.at[block(2)], x_rel.at[k], 4, x_sem.at[1, k], neighbour(turn)),
            functools.partial(send, src.at[block(3 - 2 * turn)], x_dc.at[k, 0], 5, x_sem.at[2, k], neighbour(1 - turn)),
            functools.partial(send, src.at[block(1 + 2 * turn)], x_dc.at[k, 1], 5, x_sem.at[2, k], neighbour(turn)),
            functools.partial(send, part.at[k, 1], x_in.at[k], 3, x_sem.at[0, k], across),
        )

    def x_far(k):
        return send(part.at[k, 0, block(2)], x_rel.at[k], 4, x_sem.at[1, k], far)

    started = [(axis == "y", k) for axis, k, stage in SCHEDULE if stage == 0]

    def columns(p):
        return pl.ds(started.index((p >= n_x, p - n_x if p >= n_x else p)) * wide, wide)

    def multiply(p):
        first = columns(p).start
        if first % chunk == 0:
            w_copies[first // chunk].wait_recv()
        product = jnp.dot(g2[...], w2[:, columns(p)], preferred_element_type=F32)
        part[p] = product.astype(BF16).reshape(2, half, wide)

    def x_start(k):
        multiply(k)
        x_first(k)[4]().start()

    def y_start(k):
        multiply(n_x + k)
        _, _, rel, drt, _, _ = y_first(k)
        rel().start()
        drt().start()


    def x_second(k):
        _, rel, drt, _, cross = x_first(k)
        cross().wait_recv()
        part[k, 0] = (part[k, 0].astype(F32) + x_in[k].astype(F32)).astype(BF16)
        rel().start()
        drt().start()

    def y_second(k):
        p, near, rel, _, com, _ = y_first(k)
        rel().wait_recv()
        part[p, :, block(near)] = (part[p, :, block(near)].astype(F32) + y_rel[k].astype(F32)).astype(BF16)
        com().start()


    def x_second_direct(k):
        _, _, drt, com, cross = x_first(k)
        cross().wait_recv()
        part[k, 0] = (part[k, 0].astype(F32) + x_in[k].astype(F32)).astype(BF16)
        x_far(k).start()
        drt().start()
        com().start()

    def x_last_direct(k):
        _, _, drt, com, cross = x_first(k)
        landed(x_rel.at[k], x_sem.at[1, k])
        landed(x_dc.at[k], x_sem.at[2, k])
        summed = (
            part[k, 0, block(0)].astype(F32) + x_dc[k, 0].astype(F32)
            + x_dc[k, 1].astype(F32) + x_rel[k].astype(F32)
        )
        out_ref[:, columns(k)] = summed.astype(BF16)

    def x_third(k):
        near, rel, _, com, _ = x_first(k)
        rel().wait_recv()
        part[k, 0, block(near)] = (part[k, 0, block(near)].astype(F32) + x_rel[k].astype(F32)).astype(BF16)
        com().start()

    def y_third(k):
        p, _, _, drt, com, cross = y_first(k)
        landed(y_dc.at[k], y_sem.at[1, k])
        summed = part[p, :, block(0)].astype(F32) + y_dc[k, 0].astype(F32) + y_dc[k, 1].astype(F32)
        y_out[k] = summed[1].astype(BF16)
        cross().start()
        acc[k] = summed[0]


    def x_last(k):
        _, rel, drt, com, cross = x_first(k)
        landed(x_dc.at[k], x_sem.at[2, k])
        summed = part[k, 0, block(0)].astype(F32) + x_dc[k, 0].astype(F32) + x_dc[k, 1].astype(F32)
        out_ref[:, columns(k)] = summed.astype(BF16)

    def y_last(k):
        p, _, rel, drt, com, cross = y_first(k)
        cross().wait_recv()
        out_ref[:, columns(p)] = (acc[k] + y_in[k].astype(F32)).astype(BF16)

    steps_of = {
        "x": (x_start, x_second, x_third, x_last),
        "d": (x_start, x_second_direct, x_last_direct),
        "y": (y_start, y_second, y_third, y_last),
    }
    for axis, k, stage in SCHEDULE:
        steps_of[axis][stage](k)
    for k in range(1, n_ctx):

        @pl.when(ctx + k < n_ctx)
        def _(k=k):
            state_copy(k).wait_send()

    for copy in w_copies + g_copies:
        copy.wait_send()
    for kind, whole in enumerate((y_rel, y_dc, y_in, x_in, x_rel, x_dc)):
        send(whole, whole, kind, y_sem.at[0, 0], across).wait_send()


def body(n_ctx, n_tp, in_gate, value_stream, out_gate, residues, decays, skip_gain, out_weight):
    tokens, chans = in_gate.shape
    modes = residues.shape[1]
    width = out_weight.shape[1]
    rows = tokens // n_tp
    wide = width // (X_PIECES + Y_PIECES)
    groups = chans // LANES
    hbm = pl.BlockSpec(memory_space=pltpu.HBM)
    vmem = pl.BlockSpec(memory_space=pltpu.VMEM)
    dma = pltpu.SemaphoreType.DMA
    return pl.pallas_call(
        kernel,
        out_shape=pltpu.VMEM((rows, width), BF16),
        in_specs=[hbm] * 7,
        out_specs=vmem,
        scratch_shapes=[
            pltpu.VMEM((modes, chans), F32),
            pltpu.VMEM((modes, chans), F32),
            pltpu.VMEM((1, chans), F32),
            pltpu.VMEM((tokens, chans), BF16),
            pltpu.VMEM((tokens, chans), BF16),
            pltpu.VMEM((tokens, chans), BF16),
            pltpu.VMEM((2 * chans, width), BF16),
            pltpu.VMEM((groups, tokens, LANES), F32),
            pltpu.VMEM((groups, tokens, LANES), F32),
            pltpu.VMEM((groups, modes, SUB, LANES), F32),
            pltpu.VMEM((n_ctx, modes, chans), F32),
            pltpu.VMEM((groups, tokens // 2, LANES), BF16),
            pltpu.VMEM((tokens // 2, 2 * chans), BF16),
            pltpu.VMEM((X_PIECES + Y_PIECES, 2, YS * rows, wide), BF16),
            pltpu.VMEM((X_PIECES, YS * rows, wide), BF16),
            pltpu.VMEM((X_PIECES, rows, wide), BF16),
            pltpu.VMEM((X_PIECES, 2, rows, wide), BF16),
            pltpu.VMEM((Y_PIECES, 2, rows, wide), BF16),
            pltpu.VMEM((Y_PIECES, 2, 2, rows, wide), BF16),
            pltpu.VMEM((Y_PIECES, rows, wide), BF16),
            pltpu.VMEM((Y_PIECES, rows, wide), BF16),
            pltpu.VMEM((Y_PIECES, rows, wide), F32),
            dma((7,)),
            dma((n_ctx - 1,)),
            dma((n_ctx - 1,)),
            dma((groups + W_CHUNKS,)),
            dma((groups + W_CHUNKS,)),
            dma((6,)),
            dma((3, X_PIECES)),
            dma((3, Y_PIECES)),
        ],
        compiler_params=pltpu.CompilerParams(
            collective_id=0, has_side_effects=True, vmem_limit_bytes=48 * 1024 * 1024
        ),
        cost_estimate=pl.CostEstimate(
            flops=2 * tokens * chans * width, bytes_accessed=4 * 1024 * 1024, transcendentals=0
        ),
    )(
        *(
            pltpu.with_memory_space_constraint(operand, pltpu.HBM)
            for operand in (
                in_gate, value_stream, out_gate, residues.T, decays.T, skip_gain.reshape(1, chans), out_weight
            )
        )
    )


def solution(mesh):
    n_ctx, n_tp = mesh.shape["ctx"], mesh.shape["tp"]
    in_specs = (
        P("ctx", "tp"),
        P("ctx", "tp"),
        P("ctx", "tp"),
        P("tp", None),
        P("tp", None),
        P("tp"),
        P("tp", None),
    )
    out_specs = P(("ctx", "tp"), None)
    return jax.shard_map(
        functools.partial(body, n_ctx, n_tp),
        mesh=mesh, in_specs=in_specs, out_specs=out_specs, check_vma=False,
    )
```

```python
import functools

import jax
import jax.numpy as jnp
from jax import lax
from jax.experimental import pallas as pl
from jax.experimental.pallas import tpu as pltpu
from jax.sharding import PartitionSpec as P

MESH = pl.DeviceIdType.MESH
F32 = jnp.float32
BF16 = jnp.bfloat16

LANES = 128
SUB = 8
YS = 4
W_CHUNKS = 4
X_PIECES, Y_PIECES = 7, 9

SCHEDULE = (('y', 0, 0), ('y', 1, 0), ('x', 0, 0), ('y', 2, 0), ('x', 1, 0), ('y', 3, 0), ('x', 2, 0), ('y', 4, 0), ('x', 3, 0), ('y', 5, 0), ('d', 4, 0), ('y', 6, 0), ('d', 5, 0), ('y', 7, 0), ('d', 6, 0), ('y', 8, 0), ('y', 0, 1), ('y', 1, 1), ('x', 0, 1), ('y', 2, 1), ('y', 3, 1), ('x', 1, 1), ('y', 4, 1), ('y', 5, 1), ('x', 2, 1), ('y', 6, 1), ('y', 7, 1), ('x', 3, 1), ('y', 8, 1), ('y', 0, 2), ('y', 1, 2), ('d', 4, 1), ('x', 0, 2), ('y', 2, 2), ('y', 3, 2), ('x', 1, 2), ('d', 5, 1), ('y', 4, 2), ('y', 5, 2), ('x', 2, 2), ('d', 6, 1), ('y', 6, 2), ('y', 7, 2), ('y', 0, 3), ('x', 3, 2), ('y', 1, 3), ('y', 8, 2), ('y', 2, 3), ('x', 0, 3), ('y', 3, 3), ('d', 4, 2), ('x', 1, 3), ('y', 4, 3), ('x', 2, 3), ('y', 5, 3), ('d', 5, 2), ('y', 6, 3), ('d', 6, 2), ('y', 7, 3), ('x', 3, 3), ('y', 8, 3))


def kernel(
    in_hbm, val_hbm, gate_hbm, res_hbm, dec_hbm, skip_hbm, w_hbm, out_ref,
    res_ref, dec_ref, skip_ref, ig, vs, og, w2, px, py, prefix, states, coarse, fading, g_out, g2, part,
    x_in, x_rel, x_dc, y_rel, y_dc, y_out, y_in, acc,
    load_sem, st_send, st_recv, pair_send, pair_recv, sent, x_sem, y_sem,
):
    tokens, chans = px.shape[1], px.shape[0] * LANES
    steps = tokens // SUB
    modes = res_ref.shape[0]
    n_ctx = states.shape[0]
    groups = chans // LANES
    rows = out_ref.shape[0]
    wide = part.shape[3]

    ctx = lax.axis_index("ctx")
    tp = lax.axis_index("tp")
    core = lax.rem(tp, 2)
    y = lax.rem(lax.div(tp, 2), YS)
    xh = lax.div(tp, 2 * YS)

    def device(ctx_i, xh_i, y_i, core_i):
        return (ctx_i, (xh_i * YS + y_i) * 2 + core_i)

    partner = device(ctx, xh, y, 1 - core)
    up = device(ctx, xh, lax.rem(y + 1, YS), core)
    down = device(ctx, xh, lax.rem(y + YS - 1, YS), core)
    across = device(ctx, 1 - xh, y, core)
    far = device(ctx, xh, lax.rem(y + 2, YS), core)

    small = [
        pltpu.make_async_copy(dec_hbm, dec_ref, load_sem.at[4]),
        pltpu.make_async_copy(res_hbm, res_ref, load_sem.at[5]),
        pltpu.make_async_copy(skip_hbm, skip_ref, load_sem.at[6]),
    ]
    loads = [
        pltpu.make_async_copy(in_hbm, ig, load_sem.at[0]),
        pltpu.make_async_copy(val_hbm, vs, load_sem.at[1]),
        pltpu.make_async_copy(gate_hbm, og, load_sem.at[2]),
        pltpu.make_async_copy(w_hbm, w2.at[pl.ds(0, chans)], load_sem.at[3]),
    ]
    for load in loads[:2] + small:
        load.start()
    barrier = pltpu.get_barrier_semaphore()
    peers = [partner, up, down, far, across]
    for peer in peers:
        pl.semaphore_signal(barrier, inc=1, device_id=peer, device_id_type=MESH)
    for k in range(1, n_ctx):

        @pl.when(ctx >= k)
        def _(k=k):
            pl.semaphore_signal(barrier, inc=1, device_id=(ctx - k, tp), device_id_type=MESH)

    loads[0].wait()
    loads[1].wait()
    for load in loads[2:]:
        load.start()

    for g in range(groups):
        lanes = pl.ds(g * LANES, LANES)
        product = (ig[:, lanes].astype(F32) * vs[:, lanes].astype(F32)).astype(BF16)
        px[g] = product.astype(F32)

    def spread(row):
        return jnp.broadcast_to(row, (SUB, LANES))

    position = lax.broadcasted_iota(jnp.int32, (SUB, LANES), 0)
    place = position.astype(F32)

    def group_decay(g):
        decay = dec_ref[:, pl.ds(g * LANES, LANES)]
        return decay, jnp.exp(-decay)

    for load in small:
        load.wait()

    for g in range(groups):
        lanes = pl.ds(g * LANES, LANES)
        decay, step_factor = group_decay(g)
        factors = [spread(step_factor[m : m + 1]) for m in range(modes)]

        def advance(i, held, factors=factors, g=g):
            x = px[g, pl.ds(i, SUB, stride=steps), :]
            return tuple(f * s + x for f, s in zip(factors, held))

        zero = jnp.zeros((SUB, LANES), F32)
        ends = lax.fori_loop(0, steps, advance, (zero,) * modes, unroll=8)
        for m in range(modes):
            rate = spread(decay[m : m + 1])
            tail = jnp.exp(-rate * ((SUB - 1 - place) * steps))
            states[ctx, m : m + 1, lanes] = jnp.sum(tail * ends[m], axis=0, keepdims=True)
            scan = jnp.where(position >= 1, pltpu.roll(ends[m], 1, 0), 0.0)
            for hop in (1, 2, 4):
                weight = jnp.where(position >= hop, jnp.exp(-rate * (hop * steps)), 0.0)
                scan = scan + weight * pltpu.roll(scan, hop, 0)
            prefix[g, m] = scan

    pl.semaphore_wait(barrier, len(peers) + n_ctx - 1 - ctx)

    def state_copy(k):
        return pltpu.make_async_remote_copy(
            src_ref=states.at[ctx], dst_ref=states.at[ctx],
            send_sem=st_send.at[k - 1], recv_sem=st_recv.at[k - 1],
            device_id=(lax.rem(ctx + k, n_ctx), tp), device_id_type=MESH,
        )

    for k in range(1, n_ctx):

        @pl.when(ctx + k == n_ctx // 2)
        def _(k=k):
            state_copy(k).start()

    for k in range(1, n_ctx):

        @pl.when((ctx + k < n_ctx) & (ctx + k != n_ctx // 2))
        def _(k=k):
            state_copy(k).start()

    chunk = w2.shape[1] // W_CHUNKS
    w_copies = [
        pltpu.make_async_remote_copy(
            src_ref=w_hbm.at[:, pl.ds(c * chunk, chunk)],
            dst_ref=w2.at[pl.ds(chans, chans), pl.ds(c * chunk, chunk)],
            send_sem=pair_send.at[groups + c], recv_sem=pair_recv.at[groups + c],
            device_id=partner, device_id_type=MESH,
        )
        for c in range(W_CHUNKS)
    ]
    for copy in w_copies[: W_CHUNKS // 2]:
        copy.start()

    for g in range(groups):
        lanes = pl.ds(g * LANES, LANES)
        decay, step_factor = group_decay(g)
        amplitude = res_ref[:, lanes] * jnp.sqrt(2.0 * decay)
        factors = [spread(step_factor[m : m + 1]) for m in range(modes)]
        gains = [spread(amplitude[m : m + 1]) for m in range(modes)]

        def convolve(i, held, factors=factors, gains=gains, g=g):
            rows_i = pl.ds(i, SUB, stride=steps)
            x = px[g, rows_i, :]
            held = tuple(f * s + x for f, s in zip(factors, held))
            terms = [r * s for r, s in zip(gains, held)]
            while len(terms) > 1:
                terms = [terms[j] + terms[j + 1] for j in range(0, len(terms), 2)]
            py[g, rows_i, :] = terms[0]
            return held

        lax.fori_loop(0, steps, convolve, tuple(prefix[g, m] for m in range(modes)), unroll=4)

    for g in range(groups):
        lanes = pl.ds(g * LANES, LANES)
        decay, _ = group_decay(g)
        amplitude = res_ref[:, lanes] * jnp.sqrt(2.0 * decay)
        coarse[:, lanes] = jnp.exp(-decay * float(tokens))
        for owner in range(2):
            ahead = place * steps + float(owner * rows + 1)
            for m in range(modes):
                fading[owner, g, m] = spread(amplitude[m : m + 1]) * jnp.exp(-spread(decay[m : m + 1]) * ahead)

    for k in range(1, n_ctx):

        @pl.when(ctx >= k)
        def _(k=k):
            state_copy(k).wait_recv()


    loads[2].wait()

    def target_block(r, q, core_i):
        xh_t = lax.rem(xh + q, 2)
        return (xh_t * YS + lax.rem(y + r, YS)) * 2 + core_i

    def gated_rows(block, g):
        at = pl.ds(pl.multiple_of(block * rows, rows), rows)
        lanes = pl.ds(g * LANES, LANES)
        gate = og[at, lanes].astype(F32)
        return (gate * (py[g, at, :] + skip_ref[:, lanes] * px[g, at, :])).astype(BF16)

    def carry_in(g):
        lanes = pl.ds(g * LANES, LANES)
        block_factor = coarse[:, lanes]

        def collect(i, carried):
            return block_factor * carried + states[i, :, lanes]

        return lax.fori_loop(0, ctx, collect, jnp.zeros((modes, LANES), F32))

    def extend_rows(g, carried, owner):
        _, step_factor = group_decay(g)
        first = owner * rows
        factors = [spread(step_factor[m : m + 1]) for m in range(modes)]
        fades = tuple(spread(carried[m : m + 1]) * fading[owner, g, m] for m in range(modes))

        def extend(i, fades):
            rows_i = pl.ds(first + i, SUB, stride=steps)
            terms = list(fades)
            while len(terms) > 1:
                terms = [terms[j] + terms[j + 1] for j in range(0, len(terms), 2)]
            py[g, rows_i, :] = py[g, rows_i, :] + terms[0]
            return tuple(f * v for f, v in zip(factors, fades))

        lax.fori_loop(0, rows, extend, fades, unroll=4)

    g_copies = []
    carries = []
    for g in range(groups):
        carries.append(carry_in(g))
        extend_rows(g, carries[g], 1 - core)
        for r in range(YS):
            for q in range(2):
                g_out[g, pl.ds((q * YS + r) * rows, rows), :] = gated_rows(target_block(r, q, 1 - core), g)
        g_copy = pltpu.make_async_remote_copy(
            src_ref=g_out.at[g], dst_ref=g2.at[:, pl.ds(chans + g * LANES, LANES)],
            send_sem=pair_send.at[g], recv_sem=pair_recv.at[g],
            device_id=partner, device_id_type=MESH,
        )
        g_copy.start()
        g_copies.append(g_copy)
    for copy in w_copies[W_CHUNKS // 2 :]:
        copy.start()
    for g in range(groups):
        extend_rows(g, carries[g], core)
        for r in range(YS):
            for q in range(2):
                g2[pl.ds((q * YS + r) * rows, rows), pl.ds(g * LANES, LANES)] = gated_rows(
                    target_block(r, q, core), g
                )
    loads[3].wait()
    for copy in g_copies:
        copy.wait_recv()

    half = YS * rows
    n_x, n_y = x_in.shape[0], y_in.shape[0]

    def send(src, dst, kind, sem, to):
        return pltpu.make_async_remote_copy(
            src_ref=src, dst_ref=dst, send_sem=sent.at[kind], recv_sem=sem,
            device_id=to, device_id_type=MESH,
        )

    def landed(dst, sem):
        send(dst, dst, 0, sem, across).wait_recv()

    def neighbour(turn):
        return device(ctx, xh, lax.rem(y + 1 + 2 * turn, YS), core)

    def block(r):
        return pl.ds(r * rows, rows)

    def y_first(k):
        turn = k % 2
        p = n_x + k
        src = part.at[p]
        return (
            p, 1 + 2 * turn,
            functools.partial(send, src.at[:, block(2)], y_rel.at[k], 0, y_sem.at[0, k], neighbour(turn)),
            functools.partial(send, src.at[:, block(3 - 2 * turn)], y_dc.at[k, 0], 1, y_sem.at[1, k], neighbour(1 - turn)),
            functools.partial(send, src.at[:, block(1 + 2 * turn)], y_dc.at[k, 1], 1, y_sem.at[1, k], neighbour(turn)),
            functools.partial(send, y_out.at[k], y_in.at[k], 2, y_sem.at[2, k], across),
        )

    def x_first(k):
        turn = (k + 1) % 2
        src = part.at[k, 0]
        return (
            1 + 2 * turn,
            functools.partial(send, src.at[block(2)], x_rel.at[k], 4, x_sem.at[1, k], neighbour(turn)),
            functools.partial(send, src.at[block(3 - 2 * turn)], x_dc.at[k, 0], 5, x_sem.at[2, k], neighbour(1 - turn)),
            functools.partial(send, src.at[block(1 + 2 * turn)], x_dc.at[k, 1], 5, x_sem.at[2, k], neighbour(turn)),
            functools.partial(send, part.at[k, 1], x_in.at[k], 3, x_sem.at[0, k], across),
        )

    def x_far(k):
        return send(part.at[k, 0, block(2)], x_rel.at[k], 4, x_sem.at[1, k], far)

    started = [(axis == "y", k) for axis, k, stage in SCHEDULE if stage == 0]

    def columns(p):
        return pl.ds(started.index((p >= n_x, p - n_x if p >= n_x else p)) * wide, wide)

    def multiply(p):
        first = columns(p).start
        if first % chunk == 0:
            w_copies[first // chunk].wait_recv()
        product = jnp.dot(g2[...], w2[:, columns(p)], preferred_element_type=F32)
        part[p] = product.astype(BF16).reshape(2, half, wide)

    def x_start(k):
        multiply(k)
        x_first(k)[4]().start()

    def y_start(k):
        multiply(n_x + k)
        _, _, rel, drt, _, _ = y_first(k)
        rel().start()
        drt().start()


    def x_second(k):
        _, rel, drt, _, cross = x_first(k)
        cross().wait_recv()
        part[k, 0] = (part[k, 0].astype(F32) + x_in[k].astype(F32)).astype(BF16)
        rel().start()
        drt().start()

    def y_second(k):
        p, near, rel, _, com, _ = y_first(k)
        rel().wait_recv()
        part[p, :, block(near)] = (part[p, :, block(near)].astype(F32) + y_rel[k].astype(F32)).astype(BF16)
        com().start()


    def x_second_direct(k):
        _, _, drt, com, cross = x_first(k)
        cross().wait_recv()
        part[k, 0] = (part[k, 0].astype(F32) + x_in[k].astype(F32)).astype(BF16)
        x_far(k).start()
        drt().start()
        com().start()

    def x_last_direct(k):
        _, _, drt, com, cross = x_first(k)
        landed(x_rel.at[k], x_sem.at[1, k])
        landed(x_dc.at[k], x_sem.at[2, k])
        summed = (
            part[k, 0, block(0)].astype(F32) + x_dc[k, 0].astype(F32)
            + x_dc[k, 1].astype(F32) + x_rel[k].astype(F32)
        )
        out_ref[:, columns(k)] = summed.astype(BF16)

    def x_third(k):
        near, rel, _, com, _ = x_first(k)
        rel().wait_recv()
        part[k, 0, block(near)] = (part[k, 0, block(near)].astype(F32) + x_rel[k].astype(F32)).astype(BF16)
        com().start()

    def y_third(k):
        p, _, _, drt, com, cross = y_first(k)
        landed(y_dc.at[k], y_sem.at[1, k])
        summed = part[p, :, block(0)].astype(F32) + y_dc[k, 0].astype(F32) + y_dc[k, 1].astype(F32)
        y_out[k] = summed[1].astype(BF16)
        cross().start()
        acc[k] = summed[0]


    def x_last(k):
        _, rel, drt, com, cross = x_first(k)
        landed(x_dc.at[k], x_sem.at[2, k])
        summed = part[k, 0, block(0)].astype(F32) + x_dc[k, 0].astype(F32) + x_dc[k, 1].astype(F32)
        out_ref[:, columns(k)] = summed.astype(BF16)

    def y_last(k):
        p, _, rel, drt, com, cross = y_first(k)
        cross().wait_recv()
        out_ref[:, columns(p)] = (acc[k] + y_in[k].astype(F32)).astype(BF16)

    steps_of = {
        "x": (x_start, x_second, x_third, x_last),
        "d": (x_start, x_second_direct, x_last_direct),
        "y": (y_start, y_second, y_third, y_last),
    }
    for axis, k, stage in SCHEDULE:
        steps_of[axis][stage](k)
    for k in range(1, n_ctx):

        @pl.when(ctx + k < n_ctx)
        def _(k=k):
            state_copy(k).wait_send()

    for copy in w_copies + g_copies:
        copy.wait_send()
    for kind, whole in enumerate((y_rel, y_dc, y_in, x_in, x_rel, x_dc)):
        send(whole, whole, kind, y_sem.at[0, 0], across).wait_send()


def body(n_ctx, n_tp, in_gate, value_stream, out_gate, residues, decays, skip_gain, out_weight):
    tokens, chans = in_gate.shape
    modes = residues.shape[1]
    width = out_weight.shape[1]
    rows = tokens // n_tp
    wide = width // (X_PIECES + Y_PIECES)
    groups = chans // LANES
    hbm = pl.BlockSpec(memory_space=pltpu.HBM)
    vmem = pl.BlockSpec(memory_space=pltpu.VMEM)
    dma = pltpu.SemaphoreType.DMA
    return pl.pallas_call(
        kernel,
        out_shape=pltpu.VMEM((rows, width), BF16),
        in_specs=[hbm] * 7,
        out_specs=vmem,
        scratch_shapes=[
            pltpu.VMEM((modes, chans), F32),
            pltpu.VMEM((modes, chans), F32),
            pltpu.VMEM((1, chans), F32),
            pltpu.VMEM((tokens, chans), BF16),
            pltpu.VMEM((tokens, chans), BF16),
            pltpu.VMEM((tokens, chans), BF16),
            pltpu.VMEM((2 * chans, width), BF16),
            pltpu.VMEM((groups, tokens, LANES), F32),
            pltpu.VMEM((groups, tokens, LANES), F32),
            pltpu.VMEM((groups, modes, SUB, LANES), F32),
            pltpu.VMEM((n_ctx, modes, chans), F32),
            pltpu.VMEM((modes, chans), F32),
            pltpu.VMEM((2, groups, modes, SUB, LANES), F32),
            pltpu.VMEM((groups, tokens // 2, LANES), BF16),
            pltpu.VMEM((tokens // 2, 2 * chans), BF16),
            pltpu.VMEM((X_PIECES + Y_PIECES, 2, YS * rows, wide), BF16),
            pltpu.VMEM((X_PIECES, YS * rows, wide), BF16),
            pltpu.VMEM((X_PIECES, rows, wide), BF16),
            pltpu.VMEM((X_PIECES, 2, rows, wide), BF16),
            pltpu.VMEM((Y_PIECES, 2, rows, wide), BF16),
            pltpu.VMEM((Y_PIECES, 2, 2, rows, wide), BF16),
            pltpu.VMEM((Y_PIECES, rows, wide), BF16),
            pltpu.VMEM((Y_PIECES, rows, wide), BF16),
            pltpu.VMEM((Y_PIECES, rows, wide), F32),
            dma((7,)),
            dma((n_ctx - 1,)),
            dma((n_ctx - 1,)),
            dma((groups + W_CHUNKS,)),
            dma((groups + W_CHUNKS,)),
            dma((6,)),
            dma((3, X_PIECES)),
            dma((3, Y_PIECES)),
        ],
        compiler_params=pltpu.CompilerParams(
            collective_id=0, has_side_effects=True, vmem_limit_bytes=48 * 1024 * 1024
        ),
        cost_estimate=pl.CostEstimate(
            flops=2 * tokens * chans * width, bytes_accessed=4 * 1024 * 1024, transcendentals=0
        ),
    )(
        *(
            pltpu.with_memory_space_constraint(operand, pltpu.HBM)
            for operand in (
                in_gate, value_stream, out_gate, residues.T, decays.T, skip_gain.reshape(1, chans), out_weight
            )
        )
    )


def solution(mesh):
    n_ctx, n_tp = mesh.shape["ctx"], mesh.shape["tp"]
    in_specs = (
        P("ctx", "tp"),
        P("ctx", "tp"),
        P("ctx", "tp"),
        P("tp", None),
        P("tp", None),
        P("tp"),
        P("tp", None),
    )
    out_specs = P(("ctx", "tp"), None)
    return jax.shard_map(
        functools.partial(body, n_ctx, n_tp),
        mesh=mesh, in_specs=in_specs, out_specs=out_specs, check_vma=False,
    )
```

```python
import functools

import jax
import jax.numpy as jnp
from jax import lax
from jax.experimental import pallas as pl
from jax.experimental.pallas import tpu as pltpu
from jax.sharding import PartitionSpec as P

MESH = pl.DeviceIdType.MESH
F32 = jnp.float32
BF16 = jnp.bfloat16

LANES = 128
SUB = 8
YS = 4
W_CHUNKS = 4
X_PIECES, Y_PIECES = 7, 9

SCHEDULE = (('y', 0, 0), ('y', 1, 0), ('x', 0, 0), ('y', 2, 0), ('x', 1, 0), ('y', 3, 0), ('x', 2, 0), ('y', 4, 0), ('x', 3, 0), ('y', 5, 0), ('d', 4, 0), ('y', 6, 0), ('d', 5, 0), ('y', 7, 0), ('d', 6, 0), ('y', 8, 0), ('y', 0, 1), ('y', 1, 1), ('x', 0, 1), ('y', 2, 1), ('y', 3, 1), ('x', 1, 1), ('y', 4, 1), ('y', 5, 1), ('x', 2, 1), ('y', 6, 1), ('y', 7, 1), ('x', 3, 1), ('y', 8, 1), ('y', 0, 2), ('y', 1, 2), ('d', 4, 1), ('x', 0, 2), ('y', 2, 2), ('y', 3, 2), ('x', 1, 2), ('d', 5, 1), ('y', 4, 2), ('y', 5, 2), ('x', 2, 2), ('d', 6, 1), ('y', 6, 2), ('y', 7, 2), ('y', 0, 3), ('x', 3, 2), ('y', 1, 3), ('y', 8, 2), ('y', 2, 3), ('x', 0, 3), ('y', 3, 3), ('d', 4, 2), ('x', 1, 3), ('y', 4, 3), ('x', 2, 3), ('y', 5, 3), ('d', 5, 2), ('y', 6, 3), ('d', 6, 2), ('y', 7, 3), ('x', 3, 3), ('y', 8, 3))


def kernel(
    in_hbm, val_hbm, gate_hbm, res_hbm, dec_hbm, skip_hbm, w_hbm, out_ref,
    res_ref, dec_ref, skip_ref, ig, vs, og, w2, px, py, prefix, states, coarse, fading, g_out, g2, part,
    x_in, x_rel, x_dc, y_rel, y_dc, y_out, y_in, acc,
    load_sem, st_send, st_recv, pair_send, pair_recv, sent, x_sem, y_sem,
):
    tokens, chans = px.shape[1], px.shape[0] * LANES
    steps = tokens // SUB
    modes = res_ref.shape[0]
    n_ctx = states.shape[0]
    groups = chans // LANES
    rows = out_ref.shape[0]
    wide = part.shape[3]

    ctx = lax.axis_index("ctx")
    tp = lax.axis_index("tp")
    core = lax.rem(tp, 2)
    y = lax.rem(lax.div(tp, 2), YS)
    xh = lax.div(tp, 2 * YS)

    def device(ctx_i, xh_i, y_i, core_i):
        return (ctx_i, (xh_i * YS + y_i) * 2 + core_i)

    partner = device(ctx, xh, y, 1 - core)
    up = device(ctx, xh, lax.rem(y + 1, YS), core)
    down = device(ctx, xh, lax.rem(y + YS - 1, YS), core)
    across = device(ctx, 1 - xh, y, core)
    far = device(ctx, xh, lax.rem(y + 2, YS), core)

    small = [
        pltpu.make_async_copy(dec_hbm, dec_ref, load_sem.at[4]),
        pltpu.make_async_copy(res_hbm, res_ref, load_sem.at[5]),
        pltpu.make_async_copy(skip_hbm, skip_ref, load_sem.at[6]),
    ]
    loads = [
        pltpu.make_async_copy(in_hbm, ig, load_sem.at[0]),
        pltpu.make_async_copy(val_hbm, vs, load_sem.at[1]),
        pltpu.make_async_copy(gate_hbm, og, load_sem.at[2]),
        pltpu.make_async_copy(w_hbm, w2.at[pl.ds(0, chans)], load_sem.at[3]),
    ]
    for load in loads[:2] + small:
        load.start()
    barrier = pltpu.get_barrier_semaphore()
    peers = [partner, up, down, far, across]
    for peer in peers:
        pl.semaphore_signal(barrier, inc=1, device_id=peer, device_id_type=MESH)
    for k in range(1, n_ctx):

        @pl.when(ctx >= k)
        def _(k=k):
            pl.semaphore_signal(barrier, inc=1, device_id=(ctx - k, tp), device_id_type=MESH)

    loads[0].wait()
    loads[1].wait()
    for load in loads[2:]:
        load.start()

    for g in range(groups):
        lanes = pl.ds(g * LANES, LANES)
        product = (ig[:, lanes].astype(F32) * vs[:, lanes].astype(F32)).astype(BF16)
        px[g] = product.astype(F32)

    def spread(row):
        return jnp.broadcast_to(row, (SUB, LANES))

    position = lax.broadcasted_iota(jnp.int32, (SUB, LANES), 0)
    place = position.astype(F32)

    def group_decay(g):
        decay = dec_ref[:, pl.ds(g * LANES, LANES)]
        return decay, jnp.exp(-decay)

    for load in small:
        load.wait()

    for g in range(groups):
        lanes = pl.ds(g * LANES, LANES)
        decay, step_factor = group_decay(g)
        factors = [spread(step_factor[m : m + 1]) for m in range(modes)]

        def advance(i, held, factors=factors, g=g):
            x = px[g, pl.ds(i, SUB, stride=steps), :]
            return tuple(f * s + x for f, s in zip(factors, held))

        zero = jnp.zeros((SUB, LANES), F32)
        ends = lax.fori_loop(0, steps, advance, (zero,) * modes, unroll=8)
        for m in range(modes):
            rate = spread(decay[m : m + 1])
            tail = jnp.exp(-rate * ((SUB - 1 - place) * steps))
            states[ctx, m : m + 1, lanes] = jnp.sum(tail * ends[m], axis=0, keepdims=True)
            scan = jnp.where(position >= 1, pltpu.roll(ends[m], 1, 0), 0.0)
            for hop in (1, 2, 4):
                weight = jnp.where(position >= hop, jnp.exp(-rate * (hop * steps)), 0.0)
                scan = scan + weight * pltpu.roll(scan, hop, 0)
            prefix[g, m] = scan

    pl.semaphore_wait(barrier, len(peers) + n_ctx - 1 - ctx)

    def state_copy(k):
        return pltpu.make_async_remote_copy(
            src_ref=states.at[ctx], dst_ref=states.at[ctx],
            send_sem=st_send.at[k - 1], recv_sem=st_recv.at[k - 1],
            device_id=(lax.rem(ctx + k, n_ctx), tp), device_id_type=MESH,
        )

    for k in range(1, n_ctx):

        @pl.when(ctx + k == n_ctx // 2)
        def _(k=k):
            state_copy(k).start()

    for k in range(1, n_ctx):

        @pl.when((ctx + k < n_ctx) & (ctx + k != n_ctx // 2))
        def _(k=k):
            state_copy(k).start()

    chunk = w2.shape[1] // W_CHUNKS
    w_copies = [
        pltpu.make_async_remote_copy(
            src_ref=w_hbm.at[:, pl.ds(c * chunk, chunk)],
            dst_ref=w2.at[pl.ds(chans, chans), pl.ds(c * chunk, chunk)],
            send_sem=pair_send.at[1], recv_sem=pair_recv.at[groups + c],
            device_id=partner, device_id_type=MESH,
        )
        for c in range(W_CHUNKS)
    ]
    for copy in w_copies[: W_CHUNKS // 2]:
        copy.start()

    for g in range(groups):
        lanes = pl.ds(g * LANES, LANES)
        decay, step_factor = group_decay(g)
        amplitude = res_ref[:, lanes] * jnp.sqrt(2.0 * decay)
        factors = [spread(step_factor[m : m + 1]) for m in range(modes)]
        gains = [spread(amplitude[m : m + 1]) for m in range(modes)]

        def convolve(i, held, factors=factors, gains=gains, g=g):
            rows_i = pl.ds(i, SUB, stride=steps)
            x = px[g, rows_i, :]
            held = tuple(f * s + x for f, s in zip(factors, held))
            terms = [r * s for r, s in zip(gains, held)]
            while len(terms) > 1:
                terms = [terms[j] + terms[j + 1] for j in range(0, len(terms), 2)]
            py[g, rows_i, :] = terms[0]
            return held

        lax.fori_loop(0, steps, convolve, tuple(prefix[g, m] for m in range(modes)), unroll=4)

    for g in range(groups):
        lanes = pl.ds(g * LANES, LANES)
        decay, _ = group_decay(g)
        amplitude = res_ref[:, lanes] * jnp.sqrt(2.0 * decay)
        coarse[:, lanes] = jnp.exp(-decay * float(tokens))
        for owner in range(2):
            ahead = place * steps + float(owner * rows + 1)
            for m in range(modes):
                fading[owner, g, m] = spread(amplitude[m : m + 1]) * jnp.exp(-spread(decay[m : m + 1]) * ahead)

    for k in range(1, n_ctx):

        @pl.when(ctx >= k)
        def _(k=k):
            state_copy(k).wait_recv()


    loads[2].wait()

    def target_block(r, q, core_i):
        xh_t = lax.rem(xh + q, 2)
        return (xh_t * YS + lax.rem(y + r, YS)) * 2 + core_i

    def gated_rows(block, g):
        at = pl.ds(pl.multiple_of(block * rows, rows), rows)
        lanes = pl.ds(g * LANES, LANES)
        gate = og[at, lanes].astype(F32)
        return (gate * (py[g, at, :] + skip_ref[:, lanes] * px[g, at, :])).astype(BF16)

    def carry_in(g):
        lanes = pl.ds(g * LANES, LANES)
        block_factor = coarse[:, lanes]

        def collect(i, carried):
            return block_factor * carried + states[i, :, lanes]

        return lax.fori_loop(0, ctx, collect, jnp.zeros((modes, LANES), F32))

    def extend_rows(g, carried, owner):
        _, step_factor = group_decay(g)
        first = owner * rows
        factors = [spread(step_factor[m : m + 1]) for m in range(modes)]
        fades = tuple(spread(carried[m : m + 1]) * fading[owner, g, m] for m in range(modes))

        def extend(i, fades):
            rows_i = pl.ds(first + i, SUB, stride=steps)
            terms = list(fades)
            while len(terms) > 1:
                terms = [terms[j] + terms[j + 1] for j in range(0, len(terms), 2)]
            py[g, rows_i, :] = py[g, rows_i, :] + terms[0]
            return tuple(f * v for f, v in zip(factors, fades))

        lax.fori_loop(0, rows, extend, fades, unroll=8)

    g_copies = []
    carries = []
    for g in range(groups):
        carries.append(carry_in(g))
        extend_rows(g, carries[g], 1 - core)
        for r in range(YS):
            for q in range(2):
                g_out[g, pl.ds((q * YS + r) * rows, rows), :] = gated_rows(target_block(r, q, 1 - core), g)
        g_copy = pltpu.make_async_remote_copy(
            src_ref=g_out.at[g], dst_ref=g2.at[:, pl.ds(chans + g * LANES, LANES)],
            send_sem=pair_send.at[0], recv_sem=pair_recv.at[g],
            device_id=partner, device_id_type=MESH,
        )
        g_copy.start()
        g_copies.append(g_copy)
    for copy in w_copies[W_CHUNKS // 2 :]:
        copy.start()
    for g in range(groups):
        extend_rows(g, carries[g], core)
        for r in range(YS):
            for q in range(2):
                g2[pl.ds((q * YS + r) * rows, rows), pl.ds(g * LANES, LANES)] = gated_rows(
                    target_block(r, q, core), g
                )
    loads[3].wait()
    for copy in g_copies:
        copy.wait_recv()

    half = YS * rows
    n_x, n_y = x_in.shape[0], y_in.shape[0]

    def send(src, dst, kind, sem, to):
        return pltpu.make_async_remote_copy(
            src_ref=src, dst_ref=dst, send_sem=sent.at[kind], recv_sem=sem,
            device_id=to, device_id_type=MESH,
        )

    def landed(dst, sem):
        send(dst, dst, 0, sem, across).wait_recv()

    def neighbour(turn):
        return device(ctx, xh, lax.rem(y + 1 + 2 * turn, YS), core)

    def block(r):
        return pl.ds(r * rows, rows)

    def y_first(k):
        turn = k % 2
        p = n_x + k
        src = part.at[p]
        return (
            p, 1 + 2 * turn,
            functools.partial(send, src.at[:, block(2)], y_rel.at[k], 0, y_sem.at[0, k], neighbour(turn)),
            functools.partial(send, src.at[:, block(3 - 2 * turn)], y_dc.at[k, 0], 1, y_sem.at[1, k], neighbour(1 - turn)),
            functools.partial(send, src.at[:, block(1 + 2 * turn)], y_dc.at[k, 1], 1, y_sem.at[1, k], neighbour(turn)),
            functools.partial(send, y_out.at[k], y_in.at[k], 2, y_sem.at[2, k], across),
        )

    def x_first(k):
        turn = int(k != 3)
        src = part.at[k, 0]
        return (
            1 + 2 * turn,
            functools.partial(send, src.at[block(2)], x_rel.at[k], 4, x_sem.at[1, k], neighbour(turn)),
            functools.partial(send, src.at[block(3 - 2 * turn)], x_dc.at[k, 0], 5, x_sem.at[2, k], neighbour(1 - turn)),
            functools.partial(send, src.at[block(1 + 2 * turn)], x_dc.at[k, 1], 5, x_sem.at[2, k], neighbour(turn)),
            functools.partial(send, part.at[k, 1], x_in.at[k], 3, x_sem.at[0, k], across),
        )

    def x_far(k):
        return send(part.at[k, 0, block(2)], x_rel.at[k], 4, x_sem.at[1, k], far)

    started = [(axis == "y", k) for axis, k, stage in SCHEDULE if stage == 0]

    def columns(p):
        return pl.ds(started.index((p >= n_x, p - n_x if p >= n_x else p)) * wide, wide)

    def multiply(p):
        first = columns(p).start
        if first % chunk == 0:
            w_copies[first // chunk].wait_recv()
        product = jnp.dot(g2[...], w2[:, columns(p)], preferred_element_type=F32)
        part[p] = product.astype(BF16).reshape(2, half, wide)

    def x_start(k):
        multiply(k)
        x_first(k)[4]().start()

    def y_start(k):
        multiply(n_x + k)
        _, _, rel, drt, _, _ = y_first(k)
        rel().start()
        drt().start()


    def x_second(k):
        _, rel, drt, _, cross = x_first(k)
        cross().wait_recv()
        part[k, 0] = (part[k, 0].astype(F32) + x_in[k].astype(F32)).astype(BF16)
        rel().start()
        drt().start()

    def y_second(k):
        p, near, rel, _, com, _ = y_first(k)
        rel().wait_recv()
        part[p, :, block(near)] = (part[p, :, block(near)].astype(F32) + y_rel[k].astype(F32)).astype(BF16)
        com().start()


    def x_second_direct(k):
        _, _, drt, com, cross = x_first(k)
        cross().wait_recv()
        part[k, 0] = (part[k, 0].astype(F32) + x_in[k].astype(F32)).astype(BF16)
        x_far(k).start()
        drt().start()
        com().start()

    def x_last_direct(k):
        _, _, drt, com, cross = x_first(k)
        landed(x_rel.at[k], x_sem.at[1, k])
        landed(x_dc.at[k], x_sem.at[2, k])
        summed = (
            part[k, 0, block(0)].astype(F32) + x_dc[k, 0].astype(F32)
            + x_dc[k, 1].astype(F32) + x_rel[k].astype(F32)
        )
        out_ref[:, columns(k)] = summed.astype(BF16)

    def x_third(k):
        near, rel, _, com, _ = x_first(k)
        rel().wait_recv()
        part[k, 0, block(near)] = (part[k, 0, block(near)].astype(F32) + x_rel[k].astype(F32)).astype(BF16)
        com().start()

    def y_third(k):
        p, _, _, drt, com, cross = y_first(k)
        landed(y_dc.at[k], y_sem.at[1, k])
        summed = part[p, :, block(0)].astype(F32) + y_dc[k, 0].astype(F32) + y_dc[k, 1].astype(F32)
        y_out[k] = summed[1].astype(BF16)
        cross().start()
        acc[k] = summed[0]


    def x_last(k):
        _, rel, drt, com, cross = x_first(k)
        landed(x_dc.at[k], x_sem.at[2, k])
        summed = part[k, 0, block(0)].astype(F32) + x_dc[k, 0].astype(F32) + x_dc[k, 1].astype(F32)
        out_ref[:, columns(k)] = summed.astype(BF16)

    def y_last(k):
        p, _, rel, drt, com, cross = y_first(k)
        cross().wait_recv()
        out_ref[:, columns(p)] = (acc[k] + y_in[k].astype(F32)).astype(BF16)

    steps_of = {
        "x": (x_start, x_second, x_third, x_last),
        "d": (x_start, x_second_direct, x_last_direct),
        "y": (y_start, y_second, y_third, y_last),
    }
    for axis, k, stage in SCHEDULE:
        steps_of[axis][stage](k)
    for k in range(1, n_ctx):

        @pl.when(ctx + k < n_ctx)
        def _(k=k):
            state_copy(k).wait_send()

    for whole, sem in ((g_out, pair_send.at[0]), (w2.at[pl.ds(0, chans)], pair_send.at[1])):
        pltpu.make_async_remote_copy(
            src_ref=whole, dst_ref=whole, send_sem=sem, recv_sem=pair_recv.at[0],
            device_id=partner, device_id_type=MESH,
        ).wait_send()
    for kind, whole in enumerate((y_rel, y_dc, y_in, x_in, x_rel, x_dc)):
        send(whole, whole, kind, y_sem.at[0, 0], across).wait_send()


def body(n_ctx, n_tp, in_gate, value_stream, out_gate, residues, decays, skip_gain, out_weight):
    tokens, chans = in_gate.shape
    modes = residues.shape[1]
    width = out_weight.shape[1]
    rows = tokens // n_tp
    wide = width // (X_PIECES + Y_PIECES)
    groups = chans // LANES
    hbm = pl.BlockSpec(memory_space=pltpu.HBM)
    vmem = pl.BlockSpec(memory_space=pltpu.VMEM)
    dma = pltpu.SemaphoreType.DMA
    return pl.pallas_call(
        kernel,
        out_shape=pltpu.VMEM((rows, width), BF16),
        in_specs=[hbm] * 7,
        out_specs=vmem,
        scratch_shapes=[
            pltpu.VMEM((modes, chans), F32),
            pltpu.VMEM((modes, chans), F32),
            pltpu.VMEM((1, chans), F32),
            pltpu.VMEM((tokens, chans), BF16),
            pltpu.VMEM((tokens, chans), BF16),
            pltpu.VMEM((tokens, chans), BF16),
            pltpu.VMEM((2 * chans, width), BF16),
            pltpu.VMEM((groups, tokens, LANES), F32),
            pltpu.VMEM((groups, tokens, LANES), F32),
            pltpu.VMEM((groups, modes, SUB, LANES), F32),
            pltpu.VMEM((n_ctx, modes, chans), F32),
            pltpu.VMEM((modes, chans), F32),
            pltpu.VMEM((2, groups, modes, SUB, LANES), F32),
            pltpu.VMEM((groups, tokens // 2, LANES), BF16),
            pltpu.VMEM((tokens // 2, 2 * chans), BF16),
            pltpu.VMEM((X_PIECES + Y_PIECES, 2, YS * rows, wide), BF16),
            pltpu.VMEM((X_PIECES, YS * rows, wide), BF16),
            pltpu.VMEM((X_PIECES, rows, wide), BF16),
            pltpu.VMEM((X_PIECES, 2, rows, wide), BF16),
            pltpu.VMEM((Y_PIECES, 2, rows, wide), BF16),
            pltpu.VMEM((Y_PIECES, 2, 2, rows, wide), BF16),
            pltpu.VMEM((Y_PIECES, rows, wide), BF16),
            pltpu.VMEM((Y_PIECES, rows, wide), BF16),
            pltpu.VMEM((Y_PIECES, rows, wide), F32),
            dma((7,)),
            dma((n_ctx - 1,)),
            dma((n_ctx - 1,)),
            dma((2,)),
            dma((groups + W_CHUNKS,)),
            dma((6,)),
            dma((3, X_PIECES)),
            dma((3, Y_PIECES)),
        ],
        compiler_params=pltpu.CompilerParams(
            collective_id=0, has_side_effects=True, vmem_limit_bytes=48 * 1024 * 1024
        ),
        cost_estimate=pl.CostEstimate(
            flops=2 * tokens * chans * width, bytes_accessed=4 * 1024 * 1024, transcendentals=0
        ),
    )(
        *(
            pltpu.with_memory_space_constraint(operand, pltpu.HBM)
            for operand in (
                in_gate, value_stream, out_gate, residues.T, decays.T, skip_gain.reshape(1, chans), out_weight
            )
        )
    )


def solution(mesh):
    n_ctx, n_tp = mesh.shape["ctx"], mesh.shape["tp"]
    in_specs = (
        P("ctx", "tp"),
        P("ctx", "tp"),
        P("ctx", "tp"),
        P("tp", None),
        P("tp", None),
        P("tp"),
        P("tp", None),
    )
    out_specs = P(("ctx", "tp"), None)
    return jax.shard_map(
        functools.partial(body, n_ctx, n_tp),
        mesh=mesh, in_specs=in_specs, out_specs=out_specs, check_vma=False,
    )
```

```python
import functools

import jax
import jax.numpy as jnp
from jax import lax
from jax.experimental import pallas as pl
from jax.experimental.pallas import tpu as pltpu
from jax.sharding import PartitionSpec as P

MESH = pl.DeviceIdType.MESH
F32 = jnp.float32
BF16 = jnp.bfloat16

LANES = 128
SUB = 8
YS = 4
W_CHUNKS = 4
X_PIECES, Y_PIECES = 7, 9

SCHEDULE = (('y', 0, 0), ('y', 1, 0), ('x', 0, 0), ('y', 2, 0), ('x', 1, 0), ('y', 3, 0), ('x', 2, 0), ('y', 4, 0), ('x', 3, 0), ('y', 5, 0), ('d', 4, 0), ('y', 6, 0), ('d', 5, 0), ('y', 7, 0), ('d', 6, 0), ('y', 8, 0), ('y', 0, 1), ('y', 1, 1), ('x', 0, 1), ('y', 2, 1), ('y', 3, 1), ('x', 1, 1), ('y', 4, 1), ('y', 5, 1), ('x', 2, 1), ('y', 6, 1), ('y', 7, 1), ('x', 3, 1), ('y', 8, 1), ('y', 0, 2), ('y', 1, 2), ('d', 4, 1), ('x', 0, 2), ('y', 2, 2), ('y', 3, 2), ('x', 1, 2), ('d', 5, 1), ('y', 4, 2), ('y', 5, 2), ('x', 2, 2), ('d', 6, 1), ('y', 6, 2), ('y', 7, 2), ('y', 0, 3), ('x', 3, 2), ('y', 1, 3), ('y', 8, 2), ('y', 2, 3), ('x', 0, 3), ('y', 3, 3), ('d', 4, 2), ('x', 1, 3), ('y', 4, 3), ('x', 2, 3), ('y', 5, 3), ('d', 5, 2), ('y', 6, 3), ('d', 6, 2), ('y', 7, 3), ('x', 3, 3), ('y', 8, 3))


def kernel(
    in_hbm, val_hbm, gate_hbm, res_hbm, dec_hbm, skip_hbm, w_hbm, out_ref,
    res_ref, dec_ref, skip_ref, ig, vs, og, w2, px, py, prefix, states, coarse, fading, g_out, g2, part,
    x_in, x_rel, x_dc, y_rel, y_dc, y_out, y_in, acc,
    load_sem, st_send, st_recv, pair_send, pair_recv, sent, x_sem, y_sem,
):
    tokens, chans = ig.shape
    steps = tokens // SUB
    modes = res_ref.shape[0]
    n_ctx = states.shape[0]
    groups = chans // LANES
    rows = out_ref.shape[0]
    wide = part.shape[3]

    ctx = lax.axis_index("ctx")
    tp = lax.axis_index("tp")
    core = lax.rem(tp, 2)
    y = lax.rem(lax.div(tp, 2), YS)
    xh = lax.div(tp, 2 * YS)

    def device(ctx_i, xh_i, y_i, core_i):
        return (ctx_i, (xh_i * YS + y_i) * 2 + core_i)

    partner = device(ctx, xh, y, 1 - core)
    up = device(ctx, xh, lax.rem(y + 1, YS), core)
    down = device(ctx, xh, lax.rem(y + YS - 1, YS), core)
    across = device(ctx, 1 - xh, y, core)
    far = device(ctx, xh, lax.rem(y + 2, YS), core)

    small = [
        pltpu.make_async_copy(dec_hbm, dec_ref, load_sem.at[4]),
        pltpu.make_async_copy(res_hbm, res_ref, load_sem.at[5]),
        pltpu.make_async_copy(skip_hbm, skip_ref, load_sem.at[6]),
    ]
    loads = [
        pltpu.make_async_copy(in_hbm, ig, load_sem.at[0]),
        pltpu.make_async_copy(val_hbm, vs, load_sem.at[1]),
        pltpu.make_async_copy(gate_hbm, og, load_sem.at[2]),
        pltpu.make_async_copy(w_hbm, w2.at[pl.ds(0, chans)], load_sem.at[3]),
    ]
    for load in loads[:2] + small:
        load.start()
    barrier = pltpu.get_barrier_semaphore()
    peers = [partner, up, down, far, across]
    for peer in peers:
        pl.semaphore_signal(barrier, inc=1, device_id=peer, device_id_type=MESH)
    for k in range(1, n_ctx):

        @pl.when(ctx >= k)
        def _(k=k):
            pl.semaphore_signal(barrier, inc=1, device_id=(ctx - k, tp), device_id_type=MESH)

    loads[0].wait()
    loads[1].wait()
    for load in loads[2:]:
        load.start()

    for g in range(groups):
        lanes = pl.ds(g * LANES, LANES)
        product = (ig[:, lanes].astype(F32) * vs[:, lanes].astype(F32)).astype(BF16)
        px[g, pl.ds(0, tokens), :] = product.astype(F32)

    def spread(row):
        return jnp.broadcast_to(row, (SUB, LANES))

    position = lax.broadcasted_iota(jnp.int32, (SUB, LANES), 0)
    place = position.astype(F32)

    def group_decay(g):
        decay = dec_ref[:, pl.ds(g * LANES, LANES)]
        return decay, jnp.exp(-decay)

    for load in small:
        load.wait()

    for g in range(groups):
        lanes = pl.ds(g * LANES, LANES)
        decay, step_factor = group_decay(g)
        factors = [spread(step_factor[m : m + 1]) for m in range(modes)]

        def advance(i, held, factors=factors, g=g):
            x = px[g, pl.ds(i, SUB, stride=steps), :]
            return tuple(f * s + x for f, s in zip(factors, held))

        zero = jnp.zeros((SUB, LANES), F32)
        ends = lax.fori_loop(0, steps, advance, (zero,) * modes, unroll=8)
        for m in range(modes):
            rate = spread(decay[m : m + 1])
            tail = jnp.exp(-rate * ((SUB - 1 - place) * steps))
            states[ctx, m : m + 1, lanes] = jnp.sum(tail * ends[m], axis=0, keepdims=True)
            scan = jnp.where(position >= 1, pltpu.roll(ends[m], 1, 0), 0.0)
            for hop in (1, 2, 4):
                weight = jnp.where(position >= hop, jnp.exp(-rate * (hop * steps)), 0.0)
                scan = scan + weight * pltpu.roll(scan, hop, 0)
            prefix[g, m] = scan

    pl.semaphore_wait(barrier, len(peers) + n_ctx - 1 - ctx)

    def state_copy(k):
        return pltpu.make_async_remote_copy(
            src_ref=states.at[ctx], dst_ref=states.at[ctx],
            send_sem=st_send.at[k - 1], recv_sem=st_recv.at[k - 1],
            device_id=(lax.rem(ctx + k, n_ctx), tp), device_id_type=MESH,
        )

    for k in range(1, n_ctx):

        @pl.when(ctx + k == n_ctx // 2)
        def _(k=k):
            state_copy(k).start()

    for k in range(1, n_ctx):

        @pl.when((ctx + k < n_ctx) & (ctx + k != n_ctx // 2))
        def _(k=k):
            state_copy(k).start()

    chunk = w2.shape[1] // W_CHUNKS
    w_copies = [
        pltpu.make_async_remote_copy(
            src_ref=w_hbm.at[:, pl.ds(c * chunk, chunk)],
            dst_ref=w2.at[pl.ds(chans, chans), pl.ds(c * chunk, chunk)],
            send_sem=pair_send.at[1], recv_sem=pair_recv.at[groups + c],
            device_id=partner, device_id_type=MESH,
        )
        for c in range(W_CHUNKS)
    ]
    for copy in w_copies[: W_CHUNKS // 2]:
        copy.start()

    for g in range(groups):
        lanes = pl.ds(g * LANES, LANES)
        decay, step_factor = group_decay(g)
        amplitude = res_ref[:, lanes] * jnp.sqrt(2.0 * decay)
        factors = [spread(step_factor[m : m + 1]) for m in range(modes)]
        gains = [spread(amplitude[m : m + 1]) for m in range(modes)]

        def convolve(i, held, factors=factors, gains=gains, g=g):
            rows_i = pl.ds(i, SUB, stride=steps)
            x = px[g, rows_i, :]
            held = tuple(f * s + x for f, s in zip(factors, held))
            terms = [r * s for r, s in zip(gains, held)]
            while len(terms) > 1:
                terms = [terms[j] + terms[j + 1] for j in range(0, len(terms), 2)]
            py[g, rows_i, :] = terms[0]
            return held

        lax.fori_loop(0, steps, convolve, tuple(prefix[g, m] for m in range(modes)), unroll=4)

    for g in range(groups):
        lanes = pl.ds(g * LANES, LANES)
        decay, _ = group_decay(g)
        amplitude = res_ref[:, lanes] * jnp.sqrt(2.0 * decay)
        coarse[:, lanes] = jnp.exp(-decay * float(tokens))
        for owner in range(2):
            ahead = place * steps + float(owner * rows + 1)
            for m in range(modes):
                fading[owner, g, m] = spread(amplitude[m : m + 1]) * jnp.exp(-spread(decay[m : m + 1]) * ahead)

    for k in range(1, n_ctx):

        @pl.when(ctx >= k)
        def _(k=k):
            state_copy(k).wait_recv()


    loads[2].wait()

    def target_block(r, q, core_i):
        xh_t = lax.rem(xh + q, 2)
        return (xh_t * YS + lax.rem(y + r, YS)) * 2 + core_i

    def gated_rows(block, g):
        at = pl.ds(pl.multiple_of(block * rows, rows), rows)
        lanes = pl.ds(g * LANES, LANES)
        gate = og[at, lanes].astype(F32)
        return (gate * (py[g, at, :] + skip_ref[:, lanes] * px[g, at, :])).astype(BF16)

    def carry_in(g):
        lanes = pl.ds(g * LANES, LANES)
        block_factor = coarse[:, lanes]

        def collect(i, carried):
            return block_factor * carried + states[i, :, lanes]

        return lax.fori_loop(0, ctx, collect, jnp.zeros((modes, LANES), F32))

    def extend_rows(g, carried, owner):
        _, step_factor = group_decay(g)
        first = owner * rows
        factors = [spread(step_factor[m : m + 1]) for m in range(modes)]
        fades = tuple(spread(carried[m : m + 1]) * fading[owner, g, m] for m in range(modes))

        def extend(i, fades):
            rows_i = pl.ds(first + i, SUB, stride=steps)
            terms = list(fades)
            while len(terms) > 1:
                terms = [terms[j] + terms[j + 1] for j in range(0, len(terms), 2)]
            py[g, rows_i, :] = py[g, rows_i, :] + terms[0]
            return tuple(f * v for f, v in zip(factors, fades))

        lax.fori_loop(0, rows, extend, fades, unroll=8)

    g_copies = []
    carries = []
    for g in range(groups):
        carries.append(carry_in(g))
        extend_rows(g, carries[g], 1 - core)
        for r in range(YS):
            for q in range(2):
                g_out[g, pl.ds((q * YS + r) * rows, rows), :] = gated_rows(target_block(r, q, 1 - core), g)
        g_copy = pltpu.make_async_remote_copy(
            src_ref=g_out.at[g], dst_ref=g2.at[:, pl.ds(chans + g * LANES, LANES)],
            send_sem=pair_send.at[0], recv_sem=pair_recv.at[g],
            device_id=partner, device_id_type=MESH,
        )
        g_copy.start()
        g_copies.append(g_copy)
    for copy in w_copies[W_CHUNKS // 2 :]:
        copy.start()
    for g in range(groups):
        extend_rows(g, carries[g], core)
        for r in range(YS):
            for q in range(2):
                g2[pl.ds((q * YS + r) * rows, rows), pl.ds(g * LANES, LANES)] = gated_rows(
                    target_block(r, q, core), g
                )
    loads[3].wait()
    for copy in g_copies:
        copy.wait_recv()

    half = YS * rows
    n_x, n_y = x_in.shape[0], y_in.shape[0]

    def send(src, dst, kind, sem, to):
        return pltpu.make_async_remote_copy(
            src_ref=src, dst_ref=dst, send_sem=sent.at[kind], recv_sem=sem,
            device_id=to, device_id_type=MESH,
        )

    def landed(dst, sem):
        send(dst, dst, 0, sem, across).wait_recv()

    def neighbour(turn):
        return device(ctx, xh, lax.rem(y + 1 + 2 * turn, YS), core)

    def block(r):
        return pl.ds(r * rows, rows)

    def y_first(k):
        turn = k % 2
        p = n_x + k
        src = part.at[p]
        return (
            p, 1 + 2 * turn,
            functools.partial(send, src.at[:, block(2)], y_rel.at[k], 0, y_sem.at[0, k], neighbour(turn)),
            functools.partial(send, src.at[:, block(3 - 2 * turn)], y_dc.at[k, 0], 1, y_sem.at[1, k], neighbour(1 - turn)),
            functools.partial(send, src.at[:, block(1 + 2 * turn)], y_dc.at[k, 1], 1, y_sem.at[1, k], neighbour(turn)),
            functools.partial(send, y_out.at[k], y_in.at[k], 2, y_sem.at[2, k], across),
        )

    def x_first(k):
        turn = int(k != 3)
        src = part.at[k, 0]
        return (
            1 + 2 * turn,
            functools.partial(send, src.at[block(2)], x_rel.at[k], 4, x_sem.at[1, k], neighbour(turn)),
            functools.partial(send, src.at[block(3 - 2 * turn)], x_dc.at[k, 0], 5, x_sem.at[2, k], neighbour(1 - turn)),
            functools.partial(send, src.at[block(1 + 2 * turn)], x_dc.at[k, 1], 5, x_sem.at[2, k], neighbour(turn)),
            functools.partial(send, part.at[k, 1], x_in.at[k], 3, x_sem.at[0, k], across),
        )

    def x_far(k):
        return send(part.at[k, 0, block(2)], x_rel.at[k], 4, x_sem.at[1, k], far)

    started = [(axis == "y", k) for axis, k, stage in SCHEDULE if stage == 0]

    def columns(p):
        return pl.ds(started.index((p >= n_x, p - n_x if p >= n_x else p)) * wide, wide)

    def multiply(p):
        first = columns(p).start
        if first % chunk == 0:
            w_copies[first // chunk].wait_recv()
        product = jnp.dot(g2[...], w2[:, columns(p)], preferred_element_type=F32)
        part[p] = product.astype(BF16).reshape(2, half, wide)

    def x_start(k):
        multiply(k)
        x_first(k)[4]().start()

    def y_start(k):
        multiply(n_x + k)
        _, _, rel, drt, _, _ = y_first(k)
        rel().start()
        drt().start()


    def x_second(k):
        _, rel, drt, _, cross = x_first(k)
        cross().wait_recv()
        part[k, 0] = (part[k, 0].astype(F32) + x_in[k].astype(F32)).astype(BF16)
        rel().start()
        drt().start()

    def y_second(k):
        p, near, rel, _, com, _ = y_first(k)
        rel().wait_recv()
        part[p, :, block(near)] = (part[p, :, block(near)].astype(F32) + y_rel[k].astype(F32)).astype(BF16)
        com().start()


    def x_second_direct(k):
        _, _, drt, com, cross = x_first(k)
        cross().wait_recv()
        part[k, 0] = (part[k, 0].astype(F32) + x_in[k].astype(F32)).astype(BF16)
        x_far(k).start()
        drt().start()
        com().start()

    def x_last_direct(k):
        _, _, drt, com, cross = x_first(k)
        landed(x_rel.at[k], x_sem.at[1, k])
        landed(x_dc.at[k], x_sem.at[2, k])
        summed = (
            part[k, 0, block(0)].astype(F32) + x_dc[k, 0].astype(F32)
            + x_dc[k, 1].astype(F32) + x_rel[k].astype(F32)
        )
        out_ref[:, columns(k)] = summed.astype(BF16)

    def x_third(k):
        near, rel, _, com, _ = x_first(k)
        rel().wait_recv()
        part[k, 0, block(near)] = (part[k, 0, block(near)].astype(F32) + x_rel[k].astype(F32)).astype(BF16)
        com().start()

    def y_third(k):
        p, _, _, drt, com, cross = y_first(k)
        landed(y_dc.at[k], y_sem.at[1, k])
        summed = part[p, :, block(0)].astype(F32) + y_dc[k, 0].astype(F32) + y_dc[k, 1].astype(F32)
        y_out[k] = summed[1].astype(BF16)
        cross().start()
        acc[k] = summed[0]


    def x_last(k):
        _, rel, drt, com, cross = x_first(k)
        landed(x_dc.at[k], x_sem.at[2, k])
        summed = part[k, 0, block(0)].astype(F32) + x_dc[k, 0].astype(F32) + x_dc[k, 1].astype(F32)
        out_ref[:, columns(k)] = summed.astype(BF16)

    def y_last(k):
        p, _, rel, drt, com, cross = y_first(k)
        cross().wait_recv()
        out_ref[:, columns(p)] = (acc[k] + y_in[k].astype(F32)).astype(BF16)

    steps_of = {
        "x": (x_start, x_second, x_third, x_last),
        "d": (x_start, x_second_direct, x_last_direct),
        "y": (y_start, y_second, y_third, y_last),
    }
    for axis, k, stage in SCHEDULE:
        steps_of[axis][stage](k)
    for k in range(1, n_ctx):

        @pl.when(ctx + k < n_ctx)
        def _(k=k):
            state_copy(k).wait_send()

    for whole, sem in ((g_out, pair_send.at[0]), (w2.at[pl.ds(0, chans)], pair_send.at[1])):
        pltpu.make_async_remote_copy(
            src_ref=whole, dst_ref=whole, send_sem=sem, recv_sem=pair_recv.at[0],
            device_id=partner, device_id_type=MESH,
        ).wait_send()
    for kind, whole in enumerate((y_rel, y_dc, y_in, x_in, x_rel, x_dc)):
        send(whole, whole, kind, y_sem.at[0, 0], across).wait_send()


def body(n_ctx, n_tp, in_gate, value_stream, out_gate, residues, decays, skip_gain, out_weight):
    tokens, chans = in_gate.shape
    modes = residues.shape[1]
    width = out_weight.shape[1]
    rows = tokens // n_tp
    wide = width // (X_PIECES + Y_PIECES)
    groups = chans // LANES
    hbm = pl.BlockSpec(memory_space=pltpu.HBM)
    vmem = pl.BlockSpec(memory_space=pltpu.VMEM)
    dma = pltpu.SemaphoreType.DMA
    return pl.pallas_call(
        kernel,
        out_shape=pltpu.VMEM((rows, width), BF16),
        in_specs=[hbm] * 7,
        out_specs=vmem,
        scratch_shapes=[
            pltpu.VMEM((modes, chans), F32),
            pltpu.VMEM((modes, chans), F32),
            pltpu.VMEM((1, chans), F32),
            pltpu.VMEM((tokens, chans), BF16),
            pltpu.VMEM((tokens, chans), BF16),
            pltpu.VMEM((tokens, chans), BF16),
            pltpu.VMEM((2 * chans, width), BF16),
            pltpu.VMEM((groups, tokens + tokens // SUB, LANES), F32),
            pltpu.VMEM((groups, tokens + tokens // SUB, LANES), F32),
            pltpu.VMEM((groups, modes, SUB, LANES), F32),
            pltpu.VMEM((n_ctx, modes, chans), F32),
            pltpu.VMEM((modes, chans), F32),
            pltpu.VMEM((2, groups, modes, SUB, LANES), F32),
            pltpu.VMEM((groups, tokens // 2, LANES), BF16),
            pltpu.VMEM((tokens // 2, 2 * chans), BF16),
            pltpu.VMEM((X_PIECES + Y_PIECES, 2, YS * rows, wide), BF16),
            pltpu.VMEM((X_PIECES, YS * rows, wide), BF16),
            pltpu.VMEM((X_PIECES, rows, wide), BF16),
            pltpu.VMEM((X_PIECES, 2, rows, wide), BF16),
            pltpu.VMEM((Y_PIECES, 2, rows, wide), BF16),
            pltpu.VMEM((Y_PIECES, 2, 2, rows, wide), BF16),
            pltpu.VMEM((Y_PIECES, rows, wide), BF16),
            pltpu.VMEM((Y_PIECES, rows, wide), BF16),
            pltpu.VMEM((Y_PIECES, rows, wide), F32),
            dma((7,)),
            dma((n_ctx - 1,)),
            dma((n_ctx - 1,)),
            dma((2,)),
            dma((groups + W_CHUNKS,)),
            dma((6,)),
            dma((3, X_PIECES)),
            dma((3, Y_PIECES)),
        ],
        compiler_params=pltpu.CompilerParams(
            collective_id=0, has_side_effects=True, vmem_limit_bytes=48 * 1024 * 1024
        ),
        cost_estimate=pl.CostEstimate(
            flops=2 * tokens * chans * width, bytes_accessed=4 * 1024 * 1024, transcendentals=0
        ),
    )(
        *(
            pltpu.with_memory_space_constraint(operand, pltpu.HBM)
            for operand in (
                in_gate, value_stream, out_gate, residues.T, decays.T, skip_gain.reshape(1, chans), out_weight
            )
        )
    )


def solution(mesh):
    n_ctx, n_tp = mesh.shape["ctx"], mesh.shape["tp"]
    in_specs = (
        P("ctx", "tp"),
        P("ctx", "tp"),
        P("ctx", "tp"),
        P("tp", None),
        P("tp", None),
        P("tp"),
        P("tp", None),
    )
    out_specs = P(("ctx", "tp"), None)
    return jax.shard_map(
        functools.partial(body, n_ctx, n_tp),
        mesh=mesh, in_specs=in_specs, out_specs=out_specs, check_vma=False,
    )
```
